256 devices in a mesh: seq: 16 (over x, y), head: 16 (over z, core).
Axes of the slice: x: 4, y: 4, z: 8, core: 2. Of those that a mesh axis runs over, the one named last changes fastest.
Arguments:
- video_q: bfloat16 [32768, 3072], P(('seq', 'head')), may hold values from -8 to 8
- video_k: bfloat16 [32768, 3072], P(('seq', 'head')), may hold values from -8 to 8
- video_v: bfloat16 [32768, 3072], P(('seq', 'head')), may hold values from -1.8984375 to 1.8984375
- text_q: bfloat16 [226, 3072], P(None, 'head'), may hold values from -8 to 8
- text_k: bfloat16 [226, 3072], P(None, 'head'), may hold values from -8 to 8
- text_v: bfloat16 [226, 3072], P(None, 'head'), may hold values from -1.8984375 to 1.8984375
- offsets: int32 [27, 3], replicated, may hold values from -1 to 1, as said below
- block_mask: int32 [256, 27], P('seq'), may hold values 0 or 1
- text_mask: int32 [226], replicated, may hold values from 0 to 1, as said below
Outputs:
- video_out: bfloat16 [32768, 3072], P(('seq', 'head'))
- text_out: bfloat16 [226, 3072], P(None, 'head')
The draws below stay inside these ranges and needn't reach their ends.
Inputs may be any that keep to these rules, and one draw needn't show every extreme that they name: `offsets`: each row is a distinct tile offset; a third of the rows each have time offset -1, 0 and +1. `text_mask`: text slot 0 is always live.
All inputs are finite; a program needn't handle non-finite values. No bound on the sum of `block_mask` on one device may be relied on, other than what follows from the above.
Results may differ from the reference program's by a relative error of at most 0.008.
Values may be sent and summed in bfloat16 or wider, within the bound.
No kernel may reach another device: no remote copies, remote signals or barrier semaphores. Data moves between devices by JAX's collectives and lax.ppermute only.
A program may use at most 128 MiB of HBM per device.

```python
import math
import jax
import jax.numpy as jnp
from jax import lax

HEADS = 48
HD = 64
TEXT = 226
TILE = 128
TH = 4
TW = 4
NB = 27
TT = 16
TILES = 256
TOKENS = 32768
D = 3072


def draw_video_q(key, part):
    values = jnp.clip(2.0 * jax.random.normal(jax.random.fold_in(key, 11), (TOKENS, HEADS * HD), jnp.float32), -8.0, 8.0)
    return values.astype(jnp.bfloat16)


def draw_text_q(key, part):
    values = jnp.clip(2.0 * jax.random.normal(jax.random.fold_in(key, 21), (TEXT, HEADS * HD), jnp.float32), -8.0, 8.0)
    return values.astype(jnp.bfloat16)


def draw_text_k(key, part):
    values = jnp.clip(jax.random.normal(jax.random.fold_in(key, 31), (TEXT, HEADS * HD), jnp.float32), -8.0, 8.0)
    return values.astype(jnp.bfloat16)


def draw_offsets(key, part):
    per_group = NB // 3
    blocks = []
    for shift_index in range(3):
        order = jax.random.permutation(jax.random.fold_in(key, 50 + shift_index), 9)[:per_group]
        shift_t = jnp.full((per_group,), shift_index - 1, jnp.int32)
        shift_h = (order // 3 - 1).astype(jnp.int32)
        shift_w = (order % 3 - 1).astype(jnp.int32)
        blocks.append(jnp.stack([shift_t, shift_h, shift_w], axis=1))
    return jnp.concatenate(blocks, axis=0).astype(jnp.int32)


def draw_text_mask(key, part):
    picks = jax.random.randint(jax.random.fold_in(key, 61), (TEXT,), 0, 4)
    live = jnp.where(picks < 3, 1, 0).astype(jnp.int32)
    return live.at[0].set(1).astype(jnp.int32)


def plant(array, stream_key, low, high):
    place = [jax.random.randint(jax.random.fold_in(stream_key, axis), (), 0, length) for axis, length in enumerate(array.shape)]
    main_axis = array.shape.index(max(array.shape))
    neighbour = place[:main_axis] + [(place[main_axis] + 1) % array.shape[main_axis]] + place[main_axis + 1:]
    return array.at[tuple(place)].set(low).at[tuple(neighbour)].set(high)


def steps_of(key, extent, shards, smallest, largest):
    level, own = 1.0, jax.random.fold_in(key, 6)
    for position, shards_of in shards:
        heights = jnp.exp(jax.random.uniform(jax.random.fold_in(own, position), (shards_of,), jnp.float32, smallest / len(shards), largest / len(shards)))
        level = level * jnp.repeat(heights, extent[position] // shards_of).reshape([-1 if axis == position else 1 for axis in range(len(extent))])
    return level


def centred(rng, extent, spread, most, cuts=(), kind=jnp.bfloat16):
    values = spread * jax.random.normal(rng, extent, jnp.float32)
    if cuts:
        values = values * steps_of(rng, extent, cuts, -0.22, 0.18)
    return jnp.clip(values, -most, most).astype(kind)


def setup_inputs(seed: int = 0) -> dict:
    arg_keys = jax.random.split(jax.random.key(seed), 10)
    video_q = draw_video_q(jax.random.fold_in(arg_keys[9], 71), 0)
    video_k = centred(arg_keys[1], (TOKENS, D), 1.0, 8.0, ((0, 256),))
    video_v = centred(arg_keys[2], (TOKENS, D), 0.5, 1.8984375, ((0, 256),))
    text_q = draw_text_q(jax.random.fold_in(arg_keys[9], 71), 0)
    text_k = draw_text_k(jax.random.fold_in(arg_keys[9], 71), 0)
    text_v = centred(arg_keys[5], (TEXT, D), 0.5, 1.8984375, ((1, 16),))
    offsets = draw_offsets(jax.random.fold_in(arg_keys[9], 71), 0)
    block_mask = plant((jax.random.randint(arg_keys[7], (TILES, NB), 0, 4) < 3).astype(jnp.int32), jax.random.fold_in(arg_keys[7], 1), 0, 1)
    text_mask = draw_text_mask(jax.random.fold_in(arg_keys[9], 71), 0)
    return dict(video_q=video_q, video_k=video_k, video_v=video_v, text_q=text_q, text_k=text_k, text_v=text_v, offsets=offsets, block_mask=block_mask, text_mask=text_mask)


NEG_FILL = -jnp.inf

def reference(video_q, video_k, video_v, text_q, text_k, text_v, offsets, block_mask, text_mask):
    layer_tiles = TH * TW
    feature_width = HEADS * HD
    scale = 1.0 / math.sqrt(HD)
    key_tiles = video_k.reshape(TILES, TILE, HEADS, HD)
    value_tiles = video_v.reshape(TILES, TILE, HEADS, HD)
    text_keys = text_k.reshape(TEXT, HEADS, HD).astype(jnp.float32)
    text_vals = text_v.reshape(TEXT, HEADS, HD).astype(jnp.float32)
    text_live = text_mask == 1
    tile_spots = jnp.arange(layer_tiles, dtype=jnp.int32)
    spot_height = tile_spots // TW
    spot_across = tile_spots % TW

    def one_layer(layer_index):
        queries = lax.dynamic_slice_in_dim(video_q, layer_index * (layer_tiles * TILE), layer_tiles * TILE, 0)
        queries = queries.reshape(layer_tiles, TILE, HEADS, HD).astype(jnp.float32)
        moved_t = layer_index + offsets[None, :, 0]
        moved_h = spot_height[:, None] + offsets[None, :, 1]
        moved_w = spot_across[:, None] + offsets[None, :, 2]
        mask_rows = lax.dynamic_slice_in_dim(block_mask, layer_index * layer_tiles, layer_tiles, 0)
        live = (moved_h >= 0) & (moved_h < TH) & (moved_w >= 0) & (moved_w < TW) & (moved_t >= 0) & (moved_t < TT) & (mask_rows == 1)
        target = jnp.where(live, (moved_t * TH + moved_h) * TW + moved_w, 0).astype(jnp.int32)
        nearby_k = key_tiles[target].astype(jnp.float32).reshape(layer_tiles, NB * TILE, HEADS, HD)
        nearby_v = value_tiles[target].astype(jnp.float32).reshape(layer_tiles, NB * TILE, HEADS, HD)
        live_keys = jnp.repeat(live, TILE, axis=1)
        video_scores = jnp.einsum('grhd,gkhd->ghrk', queries, nearby_k) * scale
        video_scores = jnp.where(live_keys[:, None, None, :], video_scores, NEG_FILL)
        own_scores = jnp.einsum('grhd,khd->ghrk', queries, text_keys) * scale
        own_scores = jnp.where(text_live[None, None, None, :], own_scores, NEG_FILL)
        highest = jnp.maximum(lax.optimization_barrier(jnp.max(video_scores, -1)), lax.optimization_barrier(jnp.max(own_scores, -1)))
        video_exp = jnp.exp(video_scores - highest[..., None])
        own_exp = jnp.exp(own_scores - highest[..., None])
        totals = lax.optimization_barrier(jnp.sum(video_exp, -1)) + lax.optimization_barrier(jnp.sum(own_exp, -1))
        video_weights = lax.optimization_barrier(video_exp.astype(jnp.bfloat16)).astype(jnp.float32)
        own_weights = lax.optimization_barrier(own_exp.astype(jnp.bfloat16)).astype(jnp.float32)
        mixed = jnp.einsum('ghrk,gkhd->grhd', video_weights, nearby_v) + jnp.einsum('ghrk,khd->grhd', own_weights, text_vals)
        result = mixed / jnp.transpose(totals, (0, 2, 1))[..., None]
        return result.astype(jnp.bfloat16).reshape(layer_tiles * TILE, feature_width)
    video_out = lax.map(one_layer, jnp.arange(TT, dtype=jnp.int32)).reshape(TOKENS, feature_width)
    query_heads = jnp.transpose(text_q.reshape(TEXT, HEADS, HD), (1, 0, 2))
    textk_heads = jnp.transpose(text_k.reshape(TEXT, HEADS, HD), (1, 0, 2))
    textv_heads = jnp.transpose(text_v.reshape(TEXT, HEADS, HD), (1, 0, 2))
    videok_heads = jnp.transpose(video_k.reshape(TOKENS, HEADS, HD), (1, 0, 2))
    videov_heads = jnp.transpose(video_v.reshape(TOKENS, HEADS, HD), (1, 0, 2))

    def one_head(pieces):
        head_q, head_tk, head_tv, head_vk, head_vv = pieces
        video_scores = jnp.dot(head_q, head_vk.T, preferred_element_type=jnp.float32) * scale
        own_scores = jnp.dot(head_q, head_tk.T, preferred_element_type=jnp.float32) * scale
        own_scores = jnp.where(text_live[None, :], own_scores, NEG_FILL)
        highest = jnp.maximum(lax.optimization_barrier(jnp.max(video_scores, -1)), lax.optimization_barrier(jnp.max(own_scores, -1)))
        video_exp = jnp.exp(video_scores - highest[:, None])
        own_exp = jnp.exp(own_scores - highest[:, None])
        totals = lax.optimization_barrier(jnp.sum(video_exp, -1)) + lax.optimization_barrier(jnp.sum(own_exp, -1))
        mixed = jnp.dot(video_exp.astype(jnp.bfloat16), head_vv, preferred_element_type=jnp.float32)
        mixed = mixed + jnp.dot(own_exp.astype(jnp.bfloat16), head_tv, preferred_element_type=jnp.float32)
        return (mixed / totals[:, None]).astype(jnp.bfloat16)
    text_heads = lax.map(one_head, (query_heads, textk_heads, textv_heads, videok_heads, videov_heads))
    text_out = jnp.transpose(text_heads, (1, 0, 2)).reshape(TEXT, feature_width)
    return (video_out, text_out)
```

```python
import functools
import math

import jax
import jax.numpy as jnp
from jax import lax
from jax.experimental import pallas as pl
from jax.experimental.pallas import tpu as pltpu
from jax.sharding import PartitionSpec as P

HD = 64
TEXT = 226
TEXT_ROWS = 256
TILE = 128
HALF = TILE // 2
TH = 4
TW = 4
LAYER = TH * TW
NB = 27
GROUP = 4
SLOTS = 28
LANES = 128
NEG_FILL = -jnp.inf
FACTOR = math.log2(math.e) / math.sqrt(HD)
BF16 = jnp.bfloat16
F32 = jnp.float32
VMEM_LIMIT = 56 * 1024 * 1024


def low_lanes(rows):
    return lax.broadcasted_iota(jnp.int32, (rows, LANES), 1) < HD


def swapped(block):
    return jnp.concatenate([block[:, HD:], block[:, :HD]], axis=1)


def dot_nt(a, b):
    return lax.dot_general(a, b, (((1,), (1,)), ((), ())), preferred_element_type=F32)


def dot_nn(a, b):
    return lax.dot_general(a, b, (((1,), (0,)), ((), ())), preferred_element_type=F32)


def pack_kernel(q_ref, k_ref, v_ref, single_ref, pair_kv_ref, pair_q_ref):
    low = low_lanes(HALF)
    for n, ref in enumerate((k_ref, v_ref, q_ref)):
        middle = ref[:, LANES : 2 * LANES].astype(F32)
        upper, lower = middle[:HALF], middle[HALF:]
        rows = slice(n * HALF, (n + 1) * HALF)
        single_ref[0, rows, :] = jnp.where(low, upper, swapped(lower)).astype(BF16)
        single_ref[1, rows, :] = jnp.where(low, swapped(upper), lower).astype(BF16)
        first, last = ref[:, :LANES], ref[:, 2 * LANES :]
        if n < 2:
            rows = slice(n * TILE, (n + 1) * TILE)
            pair_kv_ref[0, rows, :] = first
            pair_kv_ref[1, rows, :] = last
        else:
            pair_q_ref[0] = first
            pair_q_ref[1] = last


def pack(video_q, video_k, video_v):
    groups = video_q.shape[1] // (3 * HD)
    block = pl.BlockSpec((TILE, 3 * LANES), lambda i: (0, i))
    rows = (3 * HALF, 2 * TILE, TILE)
    return pl.pallas_call(
        pack_kernel,
        grid=(groups // 2,),
        in_specs=[block] * 3,
        out_specs=[pl.BlockSpec((2, r, LANES), lambda i: (i, 0, 0)) for r in rows],
        out_shape=[jax.ShapeDtypeStruct((groups, r, LANES), BF16) for r in rows],
        cost_estimate=pl.CostEstimate(flops=0, bytes_accessed=4 * 3 * video_q.size, transcendentals=0),
        name="pack",
    )(video_q, video_k, video_v)


def unpack_kernel(single_ref, pair_ref, out_ref):
    low = low_lanes(HALF)
    even = single_ref[0].astype(F32)
    odd = single_ref[1].astype(F32)
    out_ref[:, :LANES] = pair_ref[0]
    out_ref[:HALF, LANES : 2 * LANES] = jnp.where(low, even, swapped(odd)).astype(BF16)
    out_ref[HALF:, LANES : 2 * LANES] = jnp.where(low, swapped(even), odd).astype(BF16)
    out_ref[:, 2 * LANES :] = pair_ref[1]


def unpack(single, pair):
    groups = single.shape[0]
    return pl.pallas_call(
        unpack_kernel,
        grid=(groups // 2,),
        in_specs=[
            pl.BlockSpec((2, HALF, LANES), lambda i: (i, 0, 0)),
            pl.BlockSpec((2, TILE, LANES), lambda i: (i, 0, 0)),
        ],
        out_specs=pl.BlockSpec((TILE, 3 * LANES), lambda i: (0, i)),
        out_shape=jax.ShapeDtypeStruct((TILE, groups * 3 * HD), BF16),
        name="unpack",
    )(single, pair)


def neighbour_lists(offsets, block_mask):
    spots = jnp.arange(LAYER, dtype=jnp.int32)
    layer = lax.axis_index("seq") + offsets[None, :, 0]
    moved_h = spots[:, None] // TW + offsets[None, :, 1]
    moved_w = spots[:, None] % TW + offsets[None, :, 2]
    live = (
        (moved_h >= 0)
        & (moved_h < TH)
        & (moved_w >= 0)
        & (moved_w < TW)
        & (layer >= 0)
        & (layer < lax.axis_size("seq"))
        & (block_mask == 1)
    )
    target = ((offsets[None, :, 0] + 1) * TH + moved_h) * TW + moved_w
    ones = live.astype(jnp.int32)
    earlier = jnp.arange(NB)[:, None] < jnp.arange(NB)[None, :]
    place = jnp.sum(jnp.where(earlier[None], ones[:, :, None], 0), axis=1)
    slots = jnp.arange(SLOTS, dtype=jnp.int32)
    chosen = live[:, :, None] & (place[:, :, None] == slots[None, None, :])
    table = jnp.sum(jnp.where(chosen, target[:, :, None], 0), axis=1)
    counts = jnp.sum(ones, axis=1)
    table = jnp.where(slots[None, :] < counts[:, None], table, table[:, :1])
    return counts, table.reshape(-1)


def attend_rows(queries, text_k, text_v, text_bias, count, keys_of, values_of, score_ref, top_ref, total_ref, mixed_ref):
    scores = dot_nt(queries, text_k) + text_bias
    left, right = scores[:, :LANES], scores[:, LANES:]
    score_ref[0] = left
    score_ref[1] = right
    top_ref[...] = jnp.maximum(left, right)
    groups = (count + (GROUP - 1)) // GROUP

    def first_pass(g, carry):
        keys = jnp.concatenate([keys_of(g * GROUP + j) for j in range(GROUP)], axis=0)
        found = dot_nt(queries, keys)
        parts = [found[:, j * LANES : (j + 1) * LANES] for j in range(GROUP)]
        for j in range(GROUP):
            score_ref[2 + g * GROUP + j] = parts[j]
        top_ref[...] = jnp.maximum(
            top_ref[...], jnp.maximum(jnp.maximum(parts[0], parts[1]), jnp.maximum(parts[2], parts[3]))
        )
        return carry

    lax.fori_loop(0, groups, first_pass, 0)
    for j in range(GROUP - 1):

        @pl.when(count + j < groups * GROUP)
        def _():
            score_ref[2 + count + j] = jnp.full(score_ref.shape[1:], NEG_FILL, F32)

    highest = jnp.max(top_ref[...], axis=1, keepdims=True)
    shift = highest * FACTOR
    weights = [jnp.exp2(score_ref[j] * FACTOR - shift) for j in range(2)]
    total_ref[...] = weights[0] + weights[1]
    mixed_ref[...] = dot_nn(jnp.concatenate([w.astype(BF16) for w in weights], axis=1), text_v)

    def second_pass(g, carry):
        parts = [jnp.exp2(score_ref[2 + g * GROUP + j] * FACTOR - shift) for j in range(GROUP)]
        total_ref[...] += (parts[0] + parts[1]) + (parts[2] + parts[3])
        values = jnp.concatenate([values_of(g * GROUP + j) for j in range(GROUP)], axis=0)
        mixed_ref[...] += dot_nn(jnp.concatenate([p.astype(BF16) for p in parts], axis=1), values)
        return carry

    lax.fori_loop(0, groups, second_pass, 0)
    return highest, jnp.sum(total_ref[...], axis=1, keepdims=True)


def spread_single(packed):
    wide = packed.astype(F32)
    return jnp.concatenate([wide, swapped(wide)], axis=0).astype(BF16)


def video_kernel(
    heads, counts_ref, table_ref, q_ref, before_ref, own_ref, after_ref, text_k_ref, text_v_ref, bias_ref, out_ref,
    kv_ref, wide_ref, score_ref, top_ref, total_ref, mixed_ref, sems,
):
    copies = [
        pltpu.make_async_copy(ref, kv_ref.at[pl.ds(n * LAYER, LAYER)], sems.at[n])
        for n, ref in enumerate((before_ref, own_ref, after_ref))
    ]
    for copy in copies:
        copy.start()
    for copy in copies:
        copy.wait()
    if heads == 1:

        def widen(t, carry):
            for n in range(2):
                wide_ref[t, n * TILE : (n + 1) * TILE, :] = spread_single(kv_ref[t, n * HALF : (n + 1) * HALF, :])
            return carry

        lax.fori_loop(0, 3 * LAYER, widen, 0)
        tiles_ref = wide_ref
    else:
        tiles_ref = kv_ref

    def one_tile(i, carry):
        low = low_lanes(TILE)
        if heads == 1:
            wide = q_ref[i].astype(F32)
            block = jnp.concatenate([wide, swapped(wide)], axis=0)
            queries = jnp.where(low, block, 0.0).astype(BF16)
        else:
            block = q_ref[i].astype(F32)
            queries = jnp.concatenate([jnp.where(low, block, 0.0), jnp.where(low, 0.0, block)], axis=0).astype(BF16)
        _, total = attend_rows(
            queries,
            text_k_ref[...],
            text_v_ref[...],
            bias_ref[...],
            counts_ref[i],
            lambda slot: tiles_ref[table_ref[i * SLOTS + slot], :TILE, :],
            lambda slot: tiles_ref[table_ref[i * SLOTS + slot], TILE:, :],
            score_ref,
            top_ref,
            total_ref,
            mixed_ref,
        )
        result = mixed_ref[...] / total
        if heads == 1:
            out_ref[i] = jnp.where(low_lanes(HALF), result[:HALF], swapped(result[HALF:])).astype(BF16)
        else:
            out_ref[i] = jnp.where(low, result[:TILE], result[TILE:]).astype(BF16)
        return carry

    lax.fori_loop(0, LAYER, one_tile, 0)


def video_attention(heads, counts, table, queries, before, own, after, text_k, text_v, text_bias):
    rows = heads * TILE
    smem = pl.BlockSpec(memory_space=pltpu.SMEM)
    vmem = pl.BlockSpec(memory_space=pltpu.VMEM)
    hbm = pl.BlockSpec(memory_space=pl.ANY)
    pairs = 300 * TILE * TILE * heads
    wide_tiles = 3 * LAYER if heads == 1 else 1
    return pl.pallas_call(
        functools.partial(video_kernel, heads),
        in_specs=[smem, smem, vmem, hbm, hbm, hbm, vmem, vmem, vmem],
        out_specs=vmem,
        out_shape=jax.ShapeDtypeStruct(queries.shape, BF16),
        scratch_shapes=[
            pltpu.VMEM((3 * LAYER,) + own.shape[1:], BF16),
            pltpu.VMEM((wide_tiles, 2 * TILE, LANES), BF16),
            pltpu.VMEM((2 + SLOTS, rows, LANES), F32),
            pltpu.VMEM((rows, LANES), F32),
            pltpu.VMEM((rows, LANES), F32),
            pltpu.VMEM((rows, LANES), F32),
            pltpu.SemaphoreType.DMA((3,)),
        ],
        compiler_params=pltpu.CompilerParams(vmem_limit_bytes=VMEM_LIMIT),
        cost_estimate=pl.CostEstimate(flops=16 * HD * pairs, bytes_accessed=8 * own.size, transcendentals=pairs),
        name=f"video_attention_{heads}",
    )(counts, table, queries, before, own, after, text_k, text_v, text_bias)


def text_kernel(
    pair_q_ref, pair_kv_ref, pair_k_ref, pair_v_ref, single_q_ref, single_kv_ref, single_k_ref, single_v_ref, bias_ref,
    out_ref, wide_ref, score_ref, top_ref, total_ref, mixed_ref,
):
    def widen(t, carry):
        for n in range(2):
            wide_ref[t, n * TILE : (n + 1) * TILE, :] = spread_single(single_kv_ref[t, n * HALF : (n + 1) * HALF, :])
        return carry

    lax.fori_loop(0, LAYER, widen, 0)
    low = low_lanes(TEXT_ROWS)
    pair_q = pair_q_ref[...].astype(F32)
    single_q = single_q_ref[...].astype(F32)
    tops, totals, sums = [], [], []
    for head in range(3):
        if head < 2:
            queries = jnp.where(low if head == 0 else ~low, pair_q, 0.0).astype(BF16)
            text_k, text_v, tiles_ref = pair_k_ref[...], pair_v_ref[...], pair_kv_ref
        else:
            queries = jnp.where(low, single_q, 0.0).astype(BF16)
            text_k, text_v, tiles_ref = single_k_ref[...], single_v_ref[...], wide_ref
        highest, total = attend_rows(
            queries,
            text_k,
            text_v,
            bias_ref[...],
            LAYER,
            lambda slot: tiles_ref[slot, :TILE, :],
            lambda slot: tiles_ref[slot, TILE:, :],
            score_ref,
            top_ref,
            total_ref,
            mixed_ref,
        )
        tops.append(highest)
        totals.append(total)
        if head == 0:
            out_ref[:, :LANES] = mixed_ref[...]
        elif head == 1:
            out_ref[:, :LANES] = jnp.where(low, out_ref[:, :LANES], mixed_ref[...])
    lane = lax.broadcasted_iota(jnp.int32, (TEXT_ROWS, LANES), 1)
    last = jnp.where(low, mixed_ref[...], 0.0)
    for head in range(3):
        last = jnp.where(lane == HD + head, tops[head], last)
        last = jnp.where(lane == HD + 3 + head, totals[head], last)
    out_ref[:, LANES:] = last


def text_partial(pair_q, pair_kv, pair_k, pair_v, single_q, single_kv, single_k, single_v, bias):
    vmem = pl.BlockSpec(memory_space=pltpu.VMEM)
    pairs = 3 * TEXT_ROWS * (LAYER + 2) * TILE
    return pl.pallas_call(
        text_kernel,
        in_specs=[vmem] * 9,
        out_specs=vmem,
        out_shape=jax.ShapeDtypeStruct((TEXT_ROWS, 2 * LANES), F32),
        scratch_shapes=[
            pltpu.VMEM((LAYER, 2 * TILE, LANES), BF16),
            pltpu.VMEM((2 + LAYER, TEXT_ROWS, LANES), F32),
            pltpu.VMEM((TEXT_ROWS, LANES), F32),
            pltpu.VMEM((TEXT_ROWS, LANES), F32),
            pltpu.VMEM((TEXT_ROWS, LANES), F32),
        ],
        compiler_params=pltpu.CompilerParams(vmem_limit_bytes=VMEM_LIMIT),
        cost_estimate=pl.CostEstimate(flops=16 * HD * pairs, bytes_accessed=4 * pair_kv.size, transcendentals=pairs),
        name="text_partial",
    )(pair_q, pair_kv, pair_k, pair_v, single_q, single_kv, single_k, single_v, bias)


def combine_kernel(parts_ref, pair_ref, single_ref):
    parts = parts_ref[...]
    outs = []
    for head in range(3):
        tops = parts[:, :, LANES + HD + head : LANES + HD + head + 1]
        totals = parts[:, :, LANES + HD + 3 + head : LANES + HD + 4 + head]
        weight = jnp.exp2((tops - jnp.max(tops, axis=0, keepdims=True)) * FACTOR)
        mixed = parts[:, :, :LANES] if head < 2 else parts[:, :, LANES:]
        outs.append(jnp.sum(mixed * weight, axis=0) / jnp.sum(totals * weight, axis=0))
    low = low_lanes(outs[0].shape[0])
    pair_ref[...] = jnp.where(low, outs[0], outs[1]).astype(BF16)
    single_ref[...] = jnp.where(low, outs[2], 0.0).astype(BF16)


def combine(parts):
    rows = parts.shape[1]
    vmem = pl.BlockSpec(memory_space=pltpu.VMEM)
    return pl.pallas_call(
        combine_kernel,
        in_specs=[vmem],
        out_specs=[vmem, vmem],
        out_shape=[jax.ShapeDtypeStruct((rows, LANES), BF16)] * 2,
        name="text_combine",
    )(parts)


def exchange(blocks, axis):
    return lax.all_to_all(blocks, axis, split_axis=0, concat_axis=0, tiled=True)


def both_sides(layer):
    count = lax.axis_size("seq")
    up = [(i, i + 1) for i in range(count - 1)]
    down = [(i + 1, i) for i in range(count - 1)]
    return lax.ppermute(layer, "seq", up), lax.ppermute(layer, "seq", down)


def body(video_q, video_k, video_v, text_q, text_k, text_v, offsets, block_mask, text_mask):
    seq_count = lax.axis_size("seq")
    odd = lax.axis_index("head") % 2 == 1
    counts, table = neighbour_lists(offsets, block_mask)

    def split_text(text):
        grown = jnp.pad(text, ((0, TEXT_ROWS - TEXT), (0, 0)))
        pair = jnp.where(odd, grown[:, HD:], grown[:, : 2 * HD])
        single = jnp.where(odd, grown[:, :HD], grown[:, 2 * HD :])
        return pair, jnp.pad(single, ((0, 0), (0, LANES - HD)))

    (pair_tq, single_tq), (pair_tk, single_tk), (pair_tv, single_tv) = map(split_text, (text_q, text_k, text_v))
    text_live = jnp.pad(text_mask, (0, TEXT_ROWS - TEXT)) == 1
    bias = jnp.where(text_live, 0.0, NEG_FILL).astype(F32)[None, :]
    own_bias = jnp.where(lax.axis_index("seq") == 0, bias, NEG_FILL)

    single, pair_kv, pair_q = pack(video_q, video_k, video_v)
    single = exchange(single, "head")
    pair_kv = exchange(pair_kv, "head")
    pair_q = exchange(pair_q, "head")
    single_kv, single_q = single[:, : 2 * HALF], single[:, 2 * HALF :]
    single_before, single_after = both_sides(single_kv)
    pair_before, pair_after = both_sides(pair_kv)

    single_out = video_attention(
        1, counts, table, single_q, single_before, single_kv, single_after, single_tk, single_tv, bias
    )
    single_back = exchange(single_out, "head")
    partial = text_partial(
        pair_tq, pair_kv, pair_tk, pair_tv, single_tq, single_kv, single_tk, single_tv, own_bias
    )
    pair_out = video_attention(2, counts, table, pair_q, pair_before, pair_kv, pair_after, pair_tk, pair_tv, bias)
    pair_back = exchange(pair_out, "head")
    video_out = unpack(single_back, pair_back)

    rows = TEXT_ROWS // seq_count
    parts = exchange(partial.reshape(seq_count, rows, 2 * LANES), "seq")
    text_pair, text_single = combine(parts)
    mine = jnp.concatenate([text_pair, text_single], axis=1)
    whole = exchange(jnp.broadcast_to(mine[None], (seq_count,) + mine.shape), "seq").reshape(TEXT_ROWS, 2 * LANES)
    pair_part, single_part = whole[:TEXT, :LANES], whole[:TEXT, LANES : LANES + HD]
    text_out = jnp.where(
        odd,
        jnp.concatenate([single_part, pair_part], axis=1),
        jnp.concatenate([pair_part, single_part], axis=1),
    )
    return video_out, text_out


def solution(mesh):
    return jax.shard_map(
        body,
        mesh=mesh,
        in_specs=(
            P(("seq", "head"), None),
            P(("seq", "head"), None),
            P(("seq", "head"), None),
            P(None, "head"),
            P(None, "head"),
            P(None, "head"),
            P(),
            P("seq", None),
            P(),
        ),
        out_specs=(P(("seq", "head"), None), P(None, "head")),
        check_vma=False,
    )
```

```python
import functools
import math

import jax
import jax.numpy as jnp
from jax import lax
from jax.experimental import pallas as pl
from jax.experimental.pallas import tpu as pltpu
from jax.sharding import PartitionSpec as P

HD = 64
TEXT = 226
TEXT_ROWS = 256
TEXT_KEPT = 256
TILE = 128
TH = 4
TW = 4
LAYER = TH * TW
NB = 27
GROUP = 4
SLOTS = 28
LANES = 128
NEG_FILL = -jnp.inf
FACTOR = math.log2(math.e) / math.sqrt(HD)
BF16 = jnp.bfloat16
F32 = jnp.float32
VMEM_LIMIT = 56 * 1024 * 1024


def low_lanes(rows):
    return lax.broadcasted_iota(jnp.int32, (rows, LANES), 1) < HD


def dot_nt(a, b):
    return lax.dot_general(a, b, (((1,), (1,)), ((), ())), preferred_element_type=F32)


def dot_nn(a, b):
    return lax.dot_general(a, b, (((1,), (0,)), ((), ())), preferred_element_type=F32)


def pack_single_kernel(q_ref, k_ref, v_ref, out_ref, held_ref, sems):
    groups = out_ref.shape[0]

    def copy(n, u):
        ref = (k_ref, v_ref, q_ref)[n]
        return pltpu.make_async_copy(ref.at[:, pl.ds((3 * u + 1) * LANES, LANES)], held_ref.at[n, u], sems.at[n, u])

    parts = [(n, u) for u in range(groups // 2) for n in range(3)]
    for n, u in parts:
        copy(n, u).start()
    for n, u in parts:
        copy(n, u).wait()
        turned = jnp.transpose(held_ref[n, u])
        out_ref[2 * u, n * HD : (n + 1) * HD, :] = turned[:HD]
        out_ref[2 * u + 1, n * HD : (n + 1) * HD, :] = turned[HD:]


def pack_single(video_q, video_k, video_v):
    groups = video_q.shape[1] // (3 * HD)
    return pl.pallas_call(
        pack_single_kernel,
        in_specs=[pl.BlockSpec(memory_space=pl.ANY)] * 3,
        out_specs=pl.BlockSpec(memory_space=pltpu.VMEM),
        out_shape=jax.ShapeDtypeStruct((groups, 3 * HD, LANES), BF16),
        scratch_shapes=[
            pltpu.VMEM((3, groups // 2, TILE, LANES), BF16),
            pltpu.SemaphoreType.DMA((3, groups // 2)),
        ],
        cost_estimate=pl.CostEstimate(flops=0, bytes_accessed=4 * video_q.size, transcendentals=0),
        name="pack_single",
    )(video_q, video_k, video_v)


def pack_pair_kernel(q_ref, k_ref, v_ref, kv_ref, out_q_ref, sems):
    copies = []
    for n, ref in enumerate((k_ref, v_ref, q_ref)):
        for g in range(out_q_ref.shape[0]):
            source = ref.at[:, pl.ds((g // 2 * 3 + g % 2 * 2) * LANES, LANES)]
            target = kv_ref.at[g, pl.ds(n * TILE, TILE)] if n < 2 else out_q_ref.at[g]
            copies.append(pltpu.make_async_copy(source, target, sems.at[n, g]))
    for copy in copies:
        copy.start()
    for copy in copies:
        copy.wait()


def pack_pair(video_q, video_k, video_v):
    groups = video_q.shape[1] // (3 * HD)
    any_space = pl.BlockSpec(memory_space=pl.ANY)
    return pl.pallas_call(
        pack_pair_kernel,
        in_specs=[any_space] * 3,
        out_specs=[pl.BlockSpec(memory_space=pltpu.VMEM)] * 2,
        out_shape=[jax.ShapeDtypeStruct((groups, r, LANES), BF16) for r in (2 * TILE, TILE)],
        scratch_shapes=[pltpu.SemaphoreType.DMA((3, groups))],
        cost_estimate=pl.CostEstimate(flops=0, bytes_accessed=8 * video_q.size, transcendentals=0),
        name="pack_pair",
    )(video_q, video_k, video_v)


def unpack_kernel(single_ref, pair_ref, out_ref, held_ref, single_sems, pair_sems):
    groups = pair_ref.shape[0]

    def pair_copy(g):
        target = out_ref.at[:, pl.ds((g // 2 * 3 + g % 2 * 2) * LANES, LANES)]
        return pltpu.make_async_copy(pair_ref.at[g], target, pair_sems.at[g])

    def single_copy(u):
        return pltpu.make_async_copy(held_ref.at[u], out_ref.at[:, pl.ds((3 * u + 1) * LANES, LANES)], single_sems.at[u])

    for g in range(groups):
        pair_copy(g).start()
    for u in range(groups // 2):
        held_ref[u] = jnp.transpose(jnp.concatenate([single_ref[2 * u], single_ref[2 * u + 1]], axis=0))
        single_copy(u).start()
    for g in range(groups):
        pair_copy(g).wait()
    for u in range(groups // 2):
        single_copy(u).wait()


def unpack(single, pair):
    groups = single.shape[0]
    any_space = pl.BlockSpec(memory_space=pl.ANY)
    return pl.pallas_call(
        unpack_kernel,
        in_specs=[pl.BlockSpec(memory_space=pltpu.VMEM)] * 2,
        out_specs=any_space,
        out_shape=jax.ShapeDtypeStruct((TILE, groups * 3 * HD), BF16),
        scratch_shapes=[
            pltpu.VMEM((groups // 2, TILE, LANES), BF16),
            pltpu.SemaphoreType.DMA((groups // 2,)),
            pltpu.SemaphoreType.DMA((groups,)),
        ],
        name="unpack",
    )(single, pair)


def neighbour_lists(offsets, block_mask):
    spots = jnp.arange(LAYER, dtype=jnp.int32)
    layer = lax.axis_index("seq") + offsets[None, :, 0]
    moved_h = spots[:, None] // TW + offsets[None, :, 1]
    moved_w = spots[:, None] % TW + offsets[None, :, 2]
    live = (
        (moved_h >= 0)
        & (moved_h < TH)
        & (moved_w >= 0)
        & (moved_w < TW)
        & (layer >= 0)
        & (layer < lax.axis_size("seq"))
        & (block_mask == 1)
    )
    target = ((offsets[None, :, 0] + 1) * TH + moved_h) * TW + moved_w
    ones = live.astype(jnp.int32)
    earlier = jnp.arange(NB)[:, None] < jnp.arange(NB)[None, :]
    place = jnp.sum(jnp.where(earlier[None], ones[:, :, None], 0), axis=1)
    slots = jnp.arange(SLOTS, dtype=jnp.int32)
    chosen = live[:, :, None] & (place[:, :, None] == slots[None, None, :])
    table = jnp.sum(jnp.where(chosen, target[:, :, None], 0), axis=1)
    counts = jnp.sum(ones, axis=1)
    ahead = (counts[:, None] > counts[None, :]) | ((counts[:, None] == counts[None, :]) & (spots[:, None] < spots[None, :]))
    rank = jnp.sum(ahead.astype(jnp.int32), axis=0)
    order = jnp.sum(jnp.where(rank[:, None] == spots[None, :], spots[:, None], 0), axis=0)
    return counts, order, table.reshape(-1)


def attend_rows(units, text_bias, groups, score_ref):
    tops = []
    for n, unit in enumerate(units):
        scores = unit["score"](unit["queries"], unit["text_k"]) + text_bias
        parts = [scores[:, :LANES], scores[:, LANES:]]
        score_ref[n, 0] = parts[0]
        score_ref[n, 1] = parts[1]
        tops.append(jnp.maximum(parts[0], parts[1]))
    for g in range(groups):
        for n, unit in enumerate(units):
            keys = [unit["keys"](g * GROUP + j) for j in range(GROUP)]
            found = unit["score"](unit["queries"], jnp.concatenate(keys, axis=unit["key_axis"]))
            for j in range(GROUP):
                part = found[:, j * LANES : (j + 1) * LANES]
                if unit["bias"] is not None:
                    part = part + unit["bias"](g * GROUP + j)
                score_ref[n, 2 + g * GROUP + j] = part
                tops[n] = jnp.maximum(tops[n], part)
    highest = [jnp.max(top, axis=1, keepdims=True) for top in tops]
    shifts = [top * FACTOR for top in highest]
    totals, mixed = [], []
    for n, unit in enumerate(units):
        weights = [jnp.exp2(score_ref[n, j] * FACTOR - shifts[n]) for j in range(2)]
        totals.append(weights[0] + weights[1])
        mixed.append(unit["mix"](jnp.concatenate([w.astype(BF16) for w in weights], axis=1), unit["text_v"]))
    for g in range(groups):
        for n, unit in enumerate(units):
            weights = [jnp.exp2(score_ref[n, 2 + g * GROUP + j] * FACTOR - shifts[n]) for j in range(GROUP)]
            totals[n] = totals[n] + ((weights[0] + weights[1]) + (weights[2] + weights[3]))
            values = jnp.concatenate([unit["values"](g * GROUP + j) for j in range(GROUP)], axis=unit["value_axis"])
            mixed[n] = mixed[n] + unit["mix"](jnp.concatenate([w.astype(BF16) for w in weights], axis=1), values)
    return highest, [jnp.sum(total, axis=1, keepdims=True) for total in totals], mixed


PAIR = dict(score=dot_nt, key_axis=0, mix=dot_nn, value_axis=0)
SINGLE = dict(score=dot_nn, key_axis=1, mix=dot_nt, value_axis=1)


def video_kernel(
    heads, together, counts_ref, order_ref, table_ref, q_ref, before_ref, own_ref, after_ref, text_k_ref, text_v_ref, bias_ref,
    out_ref, kv_ref, score_ref, sems,
):
    copies = [
        pltpu.make_async_copy(ref, kv_ref.at[pl.ds(n * LAYER, LAYER)], sems.at[n])
        for n, ref in enumerate((before_ref, own_ref, after_ref))
    ]
    for copy in copies:
        copy.start()
    for copy in copies:
        copy.wait()
    rows = kv_ref.shape[1] // 2

    def unit_of(i):
        low = low_lanes(TILE)
        block = q_ref[i].astype(F32)
        if heads == 1:
            queries = jnp.transpose(block)
        else:
            queries = jnp.concatenate([jnp.where(low, block, 0.0), jnp.where(low, 0.0, block)], axis=0)
        count = counts_ref[i]
        return dict(
            SINGLE if heads == 1 else PAIR,
            queries=queries.astype(BF16),
            text_k=text_k_ref[...],
            text_v=text_v_ref[...],
            keys=lambda slot: kv_ref[table_ref[i * SLOTS + slot], :rows, :],
            values=lambda slot: kv_ref[table_ref[i * SLOTS + slot], rows:, :],
            bias=lambda slot: jnp.where(slot < count, 0.0, NEG_FILL),
        )

    def some_tiles(step, carry):
        tiles = [order_ref[step * together + n] for n in range(together)]
        longest = functools.reduce(jnp.maximum, [counts_ref[i] for i in tiles])
        for groups in range(SLOTS // GROUP + 1):

            @pl.when((longest + (GROUP - 1)) // GROUP == groups)
            def _():
                _, totals, mixed = attend_rows([unit_of(i) for i in tiles], bias_ref[...], groups, score_ref)
                for n, i in enumerate(tiles):
                    result = mixed[n] / totals[n]
                    if heads == 1:
                        out_ref[i] = jnp.transpose(result).astype(BF16)
                    else:
                        out_ref[i] = jnp.where(low_lanes(TILE), result[:TILE], result[TILE:]).astype(BF16)

        return carry

    lax.fori_loop(0, LAYER // together, some_tiles, 0)


def video_attention(heads, counts, order, table, queries, before, own, after, text_k, text_v, text_bias):
    rows = heads * TILE
    together = 2
    smem = pl.BlockSpec(memory_space=pltpu.SMEM)
    vmem = pl.BlockSpec(memory_space=pltpu.VMEM)
    hbm = pl.BlockSpec(memory_space=pl.ANY)
    pairs = 300 * TILE * TILE * heads
    return pl.pallas_call(
        functools.partial(video_kernel, heads, together),
        in_specs=[smem, smem, smem, vmem, hbm, hbm, hbm, vmem, vmem, vmem],
        out_specs=vmem,
        out_shape=jax.ShapeDtypeStruct(queries.shape, BF16),
        scratch_shapes=[
            pltpu.VMEM((3 * LAYER,) + own.shape[1:], BF16),
            pltpu.VMEM((together, 2 + SLOTS, rows, LANES), F32),
            pltpu.SemaphoreType.DMA((3,)),
        ],
        compiler_params=pltpu.CompilerParams(vmem_limit_bytes=VMEM_LIMIT),
        cost_estimate=pl.CostEstimate(flops=16 * HD * pairs, bytes_accessed=8 * own.size, transcendentals=pairs),
        name=f"video_attention_{heads}",
    )(counts, order, table, queries, before, own, after, text_k, text_v, text_bias)


def text_kernel(
    pair_q_ref, pair_kv_ref, pair_k_ref, pair_v_ref, single_q_ref, single_kv_ref, single_k_ref, single_v_ref, bias_ref,
    out_ref, score_ref,
):
    low = low_lanes(TEXT_ROWS)
    pair_q = pair_q_ref[...].astype(F32)

    def pair_unit(head):
        return dict(
            PAIR,
            queries=jnp.where(low if head == 0 else ~low, pair_q, 0.0).astype(BF16),
            text_k=pair_k_ref[...],
            text_v=pair_v_ref[...],
            keys=lambda slot: pair_kv_ref[slot, :TILE, :],
            values=lambda slot: pair_kv_ref[slot, TILE:, :],
            bias=None,
        )

    single_unit = dict(
        SINGLE,
        queries=single_q_ref[...],
        text_k=single_k_ref[...],
        text_v=single_v_ref[...],
        keys=lambda slot: single_kv_ref[slot, :HD, :],
        values=lambda slot: single_kv_ref[slot, HD:, :],
        bias=None,
    )
    tops, totals, mixed = attend_rows([pair_unit(0), pair_unit(1), single_unit], bias_ref[...], LAYER // GROUP, score_ref)
    means = [m / t for m, t in zip(mixed, totals)]
    weighs = [top * FACTOR + jnp.log2(total) for top, total in zip(tops, totals)]
    kept = out_ref.shape[0]
    out_ref[:, :LANES] = jnp.where(low, means[0], means[1])[:kept]
    out_ref[:, LANES : 2 * LANES] = jnp.where(low, weighs[0], weighs[1])[:kept]
    out_ref[:, 2 * LANES :] = jnp.concatenate([means[2], jnp.broadcast_to(weighs[2], means[2].shape)], axis=1)[:kept]


def text_partial(pair_q, pair_kv, pair_k, pair_v, single_q, single_kv, single_k, single_v, bias):
    vmem = pl.BlockSpec(memory_space=pltpu.VMEM)
    pairs = 3 * TEXT_ROWS * (LAYER + 2) * TILE
    return pl.pallas_call(
        text_kernel,
        in_specs=[vmem] * 9,
        out_specs=vmem,
        out_shape=jax.ShapeDtypeStruct((TEXT_KEPT, 3 * LANES), F32),
        scratch_shapes=[pltpu.VMEM((3, 2 + LAYER, TEXT_ROWS, LANES), F32)],
        compiler_params=pltpu.CompilerParams(vmem_limit_bytes=VMEM_LIMIT),
        cost_estimate=pl.CostEstimate(flops=16 * HD * pairs, bytes_accessed=4 * pair_kv.size, transcendentals=pairs),
        name="text_partial",
    )(pair_q, pair_kv, pair_k, pair_v, single_q, single_kv, single_k, single_v, bias)


def combine_kernel(parts_ref, pair_ref, single_ref):
    def merged(means, weighs):
        weights = jnp.exp2(weighs - jnp.max(weighs, axis=0, keepdims=True))
        return (jnp.sum(means * weights, axis=0) / jnp.sum(weights, axis=0)).astype(BF16)

    pair_ref[...] = merged(parts_ref[:, :, :LANES], parts_ref[:, :, LANES : 2 * LANES])
    single_ref[...] = merged(parts_ref[:, :, 2 * LANES : 2 * LANES + HD], parts_ref[:, :, 2 * LANES + HD :])


def combine(parts):
    slabs, rows, _ = parts.shape
    step = rows // 4
    return pl.pallas_call(
        combine_kernel,
        grid=(rows // step,),
        in_specs=[pl.BlockSpec((slabs, step, 3 * LANES), lambda i: (0, i, 0))],
        out_specs=[pl.BlockSpec((step, LANES), lambda i: (i, 0)), pl.BlockSpec((step, HD), lambda i: (i, 0))],
        out_shape=[jax.ShapeDtypeStruct((rows, LANES), BF16), jax.ShapeDtypeStruct((rows, HD), BF16)],
        name="text_combine",
    )(parts)


def exchange(blocks, axis):
    return lax.all_to_all(blocks, axis, split_axis=0, concat_axis=0, tiled=True)


def both_sides(layer):
    count = lax.axis_size("seq")
    up = [(i, i + 1) for i in range(count - 1)]
    down = [(i + 1, i) for i in range(count - 1)]
    return lax.ppermute(layer, "seq", up), lax.ppermute(layer, "seq", down)


def after(value, *others):
    return lax.optimization_barrier((value,) + others)[0]


def body(video_q, video_k, video_v, text_q, text_k, text_v, offsets, block_mask, text_mask):
    odd = lax.axis_index("head") % 2 == 1
    counts, order, table = neighbour_lists(offsets, block_mask)

    def split_text(text):
        grown = jnp.pad(text, ((0, TEXT_ROWS - TEXT), (0, 0)))
        return jnp.where(odd, grown[:, HD:], grown[:, : 2 * HD]), jnp.where(odd, grown[:, :HD], grown[:, 2 * HD :])

    (pair_tq, single_tq), (pair_tk, single_tk), (pair_tv, single_tv) = map(split_text, (text_q, text_k, text_v))
    single_tk, single_tv = single_tk.T, single_tv.T
    text_live = jnp.pad(text_mask, (0, TEXT_ROWS - TEXT)) == 1
    bias = jnp.where(text_live, 0.0, NEG_FILL).astype(F32)[None, :]
    own_bias = jnp.where(lax.axis_index("seq") == 0, bias, NEG_FILL)

    single = exchange(pack_single(video_q, video_k, video_v), "head")
    pair_kv, pair_q = pack_pair(video_q, video_k, video_v)
    pair_kv = exchange(after(pair_kv, single), "head")
    single_kv, single_q = single[:, : 2 * HD], single[:, 2 * HD :]
    single_before, single_after = both_sides(single_kv)
    single_out = video_attention(
        1, counts, order, table, single_q, single_before, single_kv, single_after, single_tk, single_tv, bias
    )
    pair_kv = after(pair_kv, single_out)
    pair_q = exchange(after(pair_q, pair_kv), "head")
    pair_before, pair_after = both_sides(pair_kv)
    partial = text_partial(
        pair_tq, pair_kv, pair_tk, pair_tv, single_tq, single_kv, single_tk, single_tv, own_bias
    )
    parts = lax.all_gather(partial, "seq")
    single_back = exchange(after(single_out, pair_q), "head")
    pair_out = video_attention(2, counts, order, table, pair_q, pair_before, pair_kv, pair_after, pair_tk, pair_tv, bias)
    pair_back = exchange(after(pair_out, single_back), "head")
    video_out = unpack(single_back, pair_back)

    pair_part, single_part = (part[:TEXT] for part in combine(parts))
    text_out = jnp.where(
        odd,
        jnp.concatenate([single_part, pair_part], axis=1),
        jnp.concatenate([pair_part, single_part], axis=1),
    )
    return video_out, text_out


def solution(mesh):
    return jax.shard_map(
        body,
        mesh=mesh,
        in_specs=(
            P(("seq", "head"), None),
            P(("seq", "head"), None),
            P(("seq", "head"), None),
            P(None, "head"),
            P(None, "head"),
            P(None, "head"),
            P(),
            P("seq", None),
            P(),
        ),
        out_specs=(P(("seq", "head"), None), P(None, "head")),
        check_vma=False,
    )
```

```python
import functools
import math

import jax
import jax.numpy as jnp
from jax import lax
from jax.experimental import pallas as pl
from jax.experimental.pallas import tpu as pltpu
from jax.sharding import PartitionSpec as P

HD = 64
TEXT = 226
TEXT_ROWS = 256
TEXT_KEPT = 232
TILE = 128
TH = 4
TW = 4
LAYER = TH * TW
NB = 27
GROUP = 4
SLOTS = 28
LANES = 128
NEG_FILL = -jnp.inf
FACTOR = math.log2(math.e) / math.sqrt(HD)
BF16 = jnp.bfloat16
F32 = jnp.float32
VMEM_LIMIT = 56 * 1024 * 1024


def low_lanes(rows):
    return lax.broadcasted_iota(jnp.int32, (rows, LANES), 1) < HD


def dot_nt(a, b):
    return lax.dot_general(a, b, (((1,), (1,)), ((), ())), preferred_element_type=F32)


def dot_nn(a, b):
    return lax.dot_general(a, b, (((1,), (0,)), ((), ())), preferred_element_type=F32)


def pack_single_kernel(q_ref, k_ref, v_ref, out_ref, held_ref, sems):
    groups = out_ref.shape[0]

    def copy(n, u):
        ref = (k_ref, v_ref, q_ref)[n]
        return pltpu.make_async_copy(ref.at[:, pl.ds((3 * u + 1) * LANES, LANES)], held_ref.at[n, u], sems.at[n, u])

    parts = [(n, u) for u in range(groups // 2) for n in range(3)]
    for n, u in parts:
        copy(n, u).start()
    for n, u in parts:
        copy(n, u).wait()
        turned = jnp.transpose(held_ref[n, u])
        out_ref[2 * u, n * HD : (n + 1) * HD, :] = turned[:HD]
        out_ref[2 * u + 1, n * HD : (n + 1) * HD, :] = turned[HD:]


def pack_single(video_q, video_k, video_v):
    groups = video_q.shape[1] // (3 * HD)
    return pl.pallas_call(
        pack_single_kernel,
        in_specs=[pl.BlockSpec(memory_space=pl.ANY)] * 3,
        out_specs=pl.BlockSpec(memory_space=pltpu.VMEM),
        out_shape=jax.ShapeDtypeStruct((groups, 3 * HD, LANES), BF16),
        scratch_shapes=[
            pltpu.VMEM((3, groups // 2, TILE, LANES), BF16),
            pltpu.SemaphoreType.DMA((3, groups // 2)),
        ],
        cost_estimate=pl.CostEstimate(flops=0, bytes_accessed=4 * video_q.size, transcendentals=0),
        name="pack_single",
    )(video_q, video_k, video_v)


def pack_pair_kernel(q_ref, k_ref, v_ref, kv_ref, out_q_ref, sems):
    copies = []
    for n, ref in enumerate((k_ref, v_ref, q_ref)):
        for g in range(out_q_ref.shape[0]):
            source = ref.at[:, pl.ds((g // 2 * 3 + g % 2 * 2) * LANES, LANES)]
            target = kv_ref.at[g, pl.ds(n * TILE, TILE)] if n < 2 else out_q_ref.at[g]
            copies.append(pltpu.make_async_copy(source, target, sems.at[n, g]))
    for copy in copies:
        copy.start()
    for copy in copies:
        copy.wait()


def pack_pair(video_q, video_k, video_v):
    groups = video_q.shape[1] // (3 * HD)
    any_space = pl.BlockSpec(memory_space=pl.ANY)
    return pl.pallas_call(
        pack_pair_kernel,
        in_specs=[any_space] * 3,
        out_specs=[pl.BlockSpec(memory_space=pltpu.VMEM)] * 2,
        out_shape=[jax.ShapeDtypeStruct((groups, r, LANES), BF16) for r in (2 * TILE, TILE)],
        scratch_shapes=[pltpu.SemaphoreType.DMA((3, groups))],
        cost_estimate=pl.CostEstimate(flops=0, bytes_accessed=8 * video_q.size, transcendentals=0),
        name="pack_pair",
    )(video_q, video_k, video_v)


def unpack_kernel(single_ref, pair_ref, out_ref, held_ref, single_sems, pair_sems):
    groups = pair_ref.shape[0]
    first = single_ref.shape[1] - HD

    def pair_copy(g):
        target = out_ref.at[:, pl.ds((g // 2 * 3 + g % 2 * 2) * LANES, LANES)]
        return pltpu.make_async_copy(pair_ref.at[g], target, pair_sems.at[g])

    def single_copy(u):
        return pltpu.make_async_copy(held_ref.at[u], out_ref.at[:, pl.ds((3 * u + 1) * LANES, LANES)], single_sems.at[u])

    for g in range(groups):
        pair_copy(g).start()
    for u in range(groups // 2):
        both = [single_ref[2 * u + n, first:, :] for n in range(2)]
        held_ref[u] = jnp.transpose(jnp.concatenate(both, axis=0))
        single_copy(u).start()
    for g in range(groups):
        pair_copy(g).wait()
    for u in range(groups // 2):
        single_copy(u).wait()


def unpack(single, pair):
    groups = single.shape[0]
    any_space = pl.BlockSpec(memory_space=pl.ANY)
    return pl.pallas_call(
        unpack_kernel,
        in_specs=[pl.BlockSpec(memory_space=pltpu.VMEM)] * 2,
        out_specs=any_space,
        out_shape=jax.ShapeDtypeStruct((TILE, groups * 3 * HD), BF16),
        scratch_shapes=[
            pltpu.VMEM((groups // 2, TILE, LANES), BF16),
            pltpu.SemaphoreType.DMA((groups // 2,)),
            pltpu.SemaphoreType.DMA((groups,)),
        ],
        name="unpack",
    )(single, pair)


def neighbour_lists(offsets, block_mask):
    spots = jnp.arange(LAYER, dtype=jnp.int32)
    layer = lax.axis_index("seq") + offsets[None, :, 0]
    moved_h = spots[:, None] // TW + offsets[None, :, 1]
    moved_w = spots[:, None] % TW + offsets[None, :, 2]
    live = (
        (moved_h >= 0)
        & (moved_h < TH)
        & (moved_w >= 0)
        & (moved_w < TW)
        & (layer >= 0)
        & (layer < lax.axis_size("seq"))
        & (block_mask == 1)
    )
    target = ((offsets[None, :, 0] + 1) * TH + moved_h) * TW + moved_w
    ones = live.astype(jnp.int32)
    earlier = jnp.arange(NB)[:, None] < jnp.arange(NB)[None, :]
    place = jnp.sum(jnp.where(earlier[None], ones[:, :, None], 0), axis=1)
    slots = jnp.arange(SLOTS, dtype=jnp.int32)
    chosen = live[:, :, None] & (place[:, :, None] == slots[None, None, :])
    table = jnp.sum(jnp.where(chosen, target[:, :, None], 0), axis=1)
    counts = jnp.sum(ones, axis=1)
    ahead = (counts[:, None] > counts[None, :]) | ((counts[:, None] == counts[None, :]) & (spots[:, None] < spots[None, :]))
    rank = jnp.sum(ahead.astype(jnp.int32), axis=0)
    order = jnp.sum(jnp.where(rank[:, None] == spots[None, :], spots[:, None], 0), axis=0)
    return counts, order, table.reshape(-1)


def attend_rows(units, text_bias, groups, score_ref):
    tops = []
    for n, unit in enumerate(units):
        scores = unit["score"](unit["queries"], unit["text_k"]) + text_bias
        parts = [scores[:, :LANES], scores[:, LANES:]]
        score_ref[n, 0] = parts[0]
        score_ref[n, 1] = parts[1]
        tops.append(jnp.maximum(parts[0], parts[1]))
    for g in range(groups):
        for n, unit in enumerate(units):
            keys = [unit["keys"](g * GROUP + j) for j in range(GROUP)]
            found = unit["score"](unit["queries"], jnp.concatenate(keys, axis=unit["key_axis"]))
            for j in range(GROUP):
                part = found[:, j * LANES : (j + 1) * LANES]
                if unit["bias"] is not None:
                    part = part + unit["bias"](g * GROUP + j)
                score_ref[n, 2 + g * GROUP + j] = part
                tops[n] = jnp.maximum(tops[n], part)
    highest = [jnp.max(top, axis=1, keepdims=True) for top in tops]
    shifts = [top * FACTOR for top in highest]
    totals, mixed = [], []
    for n, unit in enumerate(units):
        weights = [jnp.exp2(score_ref[n, j] * FACTOR - shifts[n]) for j in range(2)]
        totals.append(weights[0] + weights[1])
        mixed.append(unit["mix"](jnp.concatenate([w.astype(BF16) for w in weights], axis=1), unit["text_v"]))
    for g in range(groups):
        for n, unit in enumerate(units):
            weights = [jnp.exp2(score_ref[n, 2 + g * GROUP + j] * FACTOR - shifts[n]) for j in range(GROUP)]
            totals[n] = totals[n] + ((weights[0] + weights[1]) + (weights[2] + weights[3]))
            values = jnp.concatenate([unit["values"](g * GROUP + j) for j in range(GROUP)], axis=unit["value_axis"])
            mixed[n] = mixed[n] + unit["mix"](jnp.concatenate([w.astype(BF16) for w in weights], axis=1), values)
    return highest, [jnp.sum(total, axis=1, keepdims=True) for total in totals], mixed


PAIR = dict(score=dot_nt, key_axis=0, mix=dot_nn, value_axis=0)
SINGLE = dict(score=dot_nn, key_axis=1, mix=dot_nt, value_axis=1)


def video_kernel(
    heads, together, query_row, counts_ref, order_ref, table_ref, q_any, before_any, own_any, after_any, passing_any,
    text_k_ref, text_v_ref, bias_ref, out_ref, kv_ref, q_ref, score_ref, sems,
):
    rows = kv_ref.shape[1] // 2
    moves = [
        (before_any, kv_ref.at[pl.ds(0, LAYER)]),
        (own_any.at[:, pl.ds(0, 2 * rows)], kv_ref.at[pl.ds(LAYER, LAYER)]),
        (after_any, kv_ref.at[pl.ds(2 * LAYER, LAYER)]),
        (q_any.at[:, pl.ds(query_row, rows)], q_ref),
    ]
    if passing_any is not None:
        moves.append((passing_any, out_ref.at[:, pl.ds(0, passing_any.shape[1])]))
    copies = [pltpu.make_async_copy(source, target, sems.at[n]) for n, (source, target) in enumerate(moves)]
    for copy in copies:
        copy.start()
    for copy in copies:
        copy.wait()
    first = out_ref.shape[1] - rows

    def unit_of(i):
        low = low_lanes(TILE)
        block = q_ref[i].astype(F32)
        if heads == 1:
            queries = jnp.transpose(block)
        else:
            queries = jnp.concatenate([jnp.where(low, block, 0.0), jnp.where(low, 0.0, block)], axis=0)
        count = counts_ref[i]
        return dict(
            SINGLE if heads == 1 else PAIR,
            queries=queries.astype(BF16),
            text_k=text_k_ref[...],
            text_v=text_v_ref[...],
            keys=lambda slot: kv_ref[table_ref[i * SLOTS + slot], :rows, :],
            values=lambda slot: kv_ref[table_ref[i * SLOTS + slot], rows:, :],
            bias=lambda slot: jnp.where(slot < count, 0.0, NEG_FILL),
        )

    def some_tiles(step, carry):
        tiles = [order_ref[step * together + n] for n in range(together)]
        longest = functools.reduce(jnp.maximum, [counts_ref[i] for i in tiles])
        for groups in range(SLOTS // GROUP + 1):

            @pl.when((longest + (GROUP - 1)) // GROUP == groups)
            def _():
                _, totals, mixed = attend_rows([unit_of(i) for i in tiles], bias_ref[...], groups, score_ref)
                for n, i in enumerate(tiles):
                    result = mixed[n] / totals[n]
                    if heads == 1:
                        out_ref[i, first:, :] = jnp.transpose(result).astype(BF16)
                    else:
                        out_ref[i, first:, :] = jnp.where(low_lanes(TILE), result[:TILE], result[TILE:]).astype(BF16)

        return carry

    lax.fori_loop(0, LAYER // together, some_tiles, 0)


def video_attention(heads, lists, queries, query_row, before, own, after, passing, text_k, text_v, text_bias):
    rows = heads * HD
    together = 2
    smem = pl.BlockSpec(memory_space=pltpu.SMEM)
    vmem = pl.BlockSpec(memory_space=pltpu.VMEM)
    hbm = pl.BlockSpec(memory_space=pl.ANY)
    pairs = 300 * TILE * TILE * heads
    kernel = functools.partial(video_kernel, heads, together, query_row)
    if passing is None:
        arrays, out_rows = (), rows
        called = lambda *refs: kernel(*refs[:7], None, *refs[7:])
    else:
        arrays, out_rows = (passing,), rows + passing.shape[1]
        called = kernel
    return pl.pallas_call(
        called,
        in_specs=[smem] * 3 + [hbm] * (4 + len(arrays)) + [vmem] * 3,
        out_specs=vmem,
        out_shape=jax.ShapeDtypeStruct((LAYER, out_rows, LANES), BF16),
        scratch_shapes=[
            pltpu.VMEM((3 * LAYER, 2 * rows, LANES), BF16),
            pltpu.VMEM((LAYER, rows, LANES), BF16),
            pltpu.VMEM((together, 2 + SLOTS, heads * TILE, LANES), F32),
            pltpu.SemaphoreType.DMA((5,)),
        ],
        compiler_params=pltpu.CompilerParams(vmem_limit_bytes=VMEM_LIMIT),
        cost_estimate=pl.CostEstimate(flops=16 * HD * pairs, bytes_accessed=8 * before.size, transcendentals=pairs),
        name=f"video_attention_{heads}",
    )(*lists, queries, before, own, after, *arrays, text_k, text_v, text_bias)


def put_text(ref, means, weighs):
    kept = ref.shape[0]
    low = low_lanes(kept)
    ref[:, :LANES] = jnp.where(low, means[0][:kept], means[1][:kept])
    lane = lax.broadcasted_iota(jnp.int32, (kept, HD), 1)
    last = jnp.zeros((kept, HD), F32)
    for head in range(3):
        last = jnp.where(lane == head, weighs[head][:kept], last)
    ref[:, LANES:] = jnp.concatenate([means[2][:kept], last], axis=1)


def merge_text(refs):
    means, weighs = [], []
    for head in range(3):
        lane = LANES + HD + head
        columns = slice(0, LANES) if head < 2 else slice(LANES, LANES + HD)
        marks = [ref[:, lane : lane + 1] for ref in refs]
        top = jnp.maximum(jnp.maximum(marks[0], marks[2]), jnp.maximum(marks[1], marks[3]))
        weights = [jnp.exp2(mark - top) for mark in marks]
        total = (weights[0] + weights[2]) + (weights[1] + weights[3])
        parts = [ref[:, columns] * (weight / total) for ref, weight in zip(refs, weights)]
        means.append((parts[0] + parts[2]) + (parts[1] + parts[3]))
        weighs.append(top + jnp.log2(total))
    return means, weighs


def merge_kernel(*refs):
    put_text(refs[4], *merge_text(refs[:4]))


def last_merge_kernel(*refs):
    means, _ = merge_text(refs[:4])
    pair_ref, single_ref = refs[4:]
    pair_ref[...] = jnp.where(low_lanes(means[0].shape[0]), means[0], means[1]).astype(BF16)
    single_ref[...] = means[2].astype(BF16)


def merge(parts, last):
    vmem = pl.BlockSpec(memory_space=pltpu.VMEM)
    rows = parts[0].shape[0]
    return pl.pallas_call(
        last_merge_kernel if last else merge_kernel,
        in_specs=[vmem] * 4,
        out_specs=[vmem] * 2 if last else vmem,
        out_shape=[jax.ShapeDtypeStruct((rows, n), BF16) for n in (LANES, HD)] if last else parts[0],
        name="text_merge",
    )(*parts)


def from_others(part, stride):
    count = lax.axis_size("seq")
    ring = 4 * stride
    parts = [part]
    for step in range(1, 4):
        pairs = [(i, i // ring * ring + (i + step * stride) % ring) for i in range(count)]
        parts.append(lax.ppermute(part, "seq", pairs))
    return parts


def text_kernel(
    pair_q_ref, pair_kv_ref, pair_k_ref, pair_v_ref, single_q_ref, single_kv_ref, single_k_ref, single_v_ref, bias_ref,
    out_ref, score_ref,
):
    low = low_lanes(TEXT_ROWS)
    pair_q = pair_q_ref[...].astype(F32)

    def pair_unit(head):
        return dict(
            PAIR,
            queries=jnp.where(low if head == 0 else ~low, pair_q, 0.0).astype(BF16),
            text_k=pair_k_ref[...],
            text_v=pair_v_ref[...],
            keys=lambda slot: pair_kv_ref[slot, :TILE, :],
            values=lambda slot: pair_kv_ref[slot, TILE:, :],
            bias=None,
        )

    single_unit = dict(
        SINGLE,
        queries=single_q_ref[...],
        text_k=single_k_ref[...],
        text_v=single_v_ref[...],
        keys=lambda slot: single_kv_ref[slot, :HD, :],
        values=lambda slot: single_kv_ref[slot, HD : 2 * HD, :],
        bias=None,
    )
    tops, totals, mixed = attend_rows([pair_unit(0), pair_unit(1), single_unit], bias_ref[...], LAYER // GROUP, score_ref)
    means = [m / t for m, t in zip(mixed, totals)]
    weighs = [top * FACTOR + jnp.log2(total) for top, total in zip(tops, totals)]
    put_text(out_ref, means, weighs)


def text_partial(pair_q, pair_kv, pair_k, pair_v, single_q, single_kv, single_k, single_v, bias):
    vmem = pl.BlockSpec(memory_space=pltpu.VMEM)
    pairs = 3 * TEXT_ROWS * (LAYER + 2) * TILE
    return pl.pallas_call(
        text_kernel,
        in_specs=[vmem] * 9,
        out_specs=vmem,
        out_shape=jax.ShapeDtypeStruct((TEXT_KEPT, 2 * LANES), F32),
        scratch_shapes=[pltpu.VMEM((3, 2 + LAYER, TEXT_ROWS, LANES), F32)],
        compiler_params=pltpu.CompilerParams(vmem_limit_bytes=VMEM_LIMIT),
        cost_estimate=pl.CostEstimate(flops=16 * HD * pairs, bytes_accessed=4 * pair_kv.size, transcendentals=pairs),
        name="text_partial",
    )(pair_q, pair_kv, pair_k, pair_v, single_q, single_kv, single_k, single_v, bias)


def exchange(blocks, axis):
    return lax.all_to_all(blocks, axis, split_axis=0, concat_axis=0, tiled=True)


def both_sides(layer):
    count = lax.axis_size("seq")
    up = [(i, i + 1) for i in range(count - 1)]
    down = [(i + 1, i) for i in range(count - 1)]
    return lax.ppermute(layer, "seq", up), lax.ppermute(layer, "seq", down)


def after(value, *others):
    return lax.optimization_barrier((value,) + others)[0]


def body(video_q, video_k, video_v, text_q, text_k, text_v, offsets, block_mask, text_mask):
    odd = lax.axis_index("head") % 2 == 1

    def split_text(text):
        grown = jnp.pad(text, ((0, TEXT_ROWS - TEXT), (0, 0)))
        return jnp.where(odd, grown[:, HD:], grown[:, : 2 * HD]), jnp.where(odd, grown[:, :HD], grown[:, 2 * HD :])

    (pair_tq, single_tq), (pair_tk, single_tk), (pair_tv, single_tv) = map(split_text, (text_q, text_k, text_v))
    single_tk, single_tv = single_tk.T, single_tv.T
    text_live = jnp.pad(text_mask, (0, TEXT_ROWS - TEXT)) == 1
    bias = jnp.where(text_live, 0.0, NEG_FILL).astype(F32)[None, :]
    own_bias = jnp.where(lax.axis_index("seq") == 0, bias, NEG_FILL)

    lists = neighbour_lists(offsets, block_mask)
    single = exchange(pack_single(video_q, video_k, video_v), "head")
    single = after(single, *lists)
    pair_kv, pair_q = pack_pair(video_q, video_k, video_v)
    pair_kv = exchange(after(pair_kv, single), "head")
    single_before, single_after = both_sides(single[:, : 2 * HD])
    mixed = video_attention(
        1, lists, single, 2 * HD, single_before, single, single_after, pair_q, single_tk, single_tv, bias
    )
    pair_kv = after(pair_kv, mixed)
    mixed = exchange(after(mixed, pair_kv), "head")
    pair_before, pair_after = both_sides(pair_kv)
    partial = text_partial(pair_tq, pair_kv, pair_tk, pair_tv, single_tq, single, single_tk, single_tv, own_bias)
    partial = merge(from_others(partial, 4), False)
    mixed = after(mixed, partial)
    pair_out = video_attention(2, lists, mixed, 0, pair_before, pair_kv, pair_after, None, pair_tk, pair_tv, bias)
    video_out = unpack(mixed, exchange(pair_out, "head"))

    pair_part, single_part = (part[:TEXT] for part in merge(from_others(partial, 1), True))
    text_out = jnp.where(
        odd,
        jnp.concatenate([single_part, pair_part], axis=1),
        jnp.concatenate([pair_part, single_part], axis=1),
    )
    return video_out, text_out


def solution(mesh):
    return jax.shard_map(
        body,
        mesh=mesh,
        in_specs=(
            P(("seq", "head"), None),
            P(("seq", "head"), None),
            P(("seq", "head"), None),
            P(None, "head"),
            P(None, "head"),
            P(None, "head"),
            P(),
            P("seq", None),
            P(),
        ),
        out_specs=(P(("seq", "head"), None), P(None, "head")),
        check_vma=False,
    )
```

```python
import functools
import math

import jax
import jax.numpy as jnp
from jax import lax
from jax.experimental import pallas as pl
from jax.experimental.pallas import tpu as pltpu
from jax.sharding import PartitionSpec as P

HD = 64
TEXT = 226
TEXT_ROWS = 256
TEXT_KEPT = 232
TILE = 128
TH = 4
TW = 4
LAYER = TH * TW
NB = 27
GROUP = 4
SLOTS = 28
LANES = 128
NEG_FILL = -jnp.inf
FACTOR = math.log2(math.e) / math.sqrt(HD)
BF16 = jnp.bfloat16
F32 = jnp.float32
VMEM_LIMIT = 56 * 1024 * 1024


def low_lanes(rows):
    return lax.broadcasted_iota(jnp.int32, (rows, LANES), 1) < HD


def dot_nt(a, b):
    return lax.dot_general(a, b, (((1,), (1,)), ((), ())), preferred_element_type=F32)


def dot_nn(a, b):
    return lax.dot_general(a, b, (((1,), (0,)), ((), ())), preferred_element_type=F32)


def pack_kernel(*refs):
    count = len(refs) - 3
    arrays, (out_ref, held_ref, sems) = refs[:count], refs[count:]
    groups = out_ref.shape[0]

    def single_copy(n, u):
        source = arrays[n].at[:, pl.ds((3 * u + 1) * LANES, LANES)]
        return pltpu.make_async_copy(source, held_ref.at[n, u], sems.at[n, groups + u])

    def pair_copy(n, g):
        source = arrays[n].at[:, pl.ds((g // 2 * 3 + g % 2 * 2) * LANES, LANES)]
        return pltpu.make_async_copy(source, out_ref.at[g, pl.ds(count * HD + n * TILE, TILE)], sems.at[n, g])

    singles = [(n, u) for u in range(groups // 2) for n in range(count)]
    pairs = [(n, g) for g in range(groups) for n in range(count)]
    for n, u in singles:
        single_copy(n, u).start()
    for n, g in pairs:
        pair_copy(n, g).start()
    for n, u in singles:
        single_copy(n, u).wait()
        turned = jnp.transpose(held_ref[n, u])
        out_ref[2 * u, n * HD : (n + 1) * HD, :] = turned[:HD]
        out_ref[2 * u + 1, n * HD : (n + 1) * HD, :] = turned[HD:]
    for n, g in pairs:
        pair_copy(n, g).wait()


def pack(*arrays):
    count = len(arrays)
    groups = arrays[0].shape[1] // (3 * HD)
    return pl.pallas_call(
        pack_kernel,
        in_specs=[pl.BlockSpec(memory_space=pl.ANY)] * count,
        out_specs=pl.BlockSpec(memory_space=pltpu.VMEM),
        out_shape=jax.ShapeDtypeStruct((groups, count * 3 * HD, LANES), BF16),
        scratch_shapes=[
            pltpu.VMEM((count, groups // 2, TILE, LANES), BF16),
            pltpu.SemaphoreType.DMA((count, groups + groups // 2)),
        ],
        cost_estimate=pl.CostEstimate(flops=0, bytes_accessed=4 * count * arrays[0].size, transcendentals=0),
        name="pack",
    )(*arrays)


def take_pair_kernel(kv_ref, token_ref, out_ref, sem):
    del token_ref
    copy = pltpu.make_async_copy(kv_ref.at[:, pl.ds(2 * HD, 2 * TILE)], out_ref, sem)
    copy.start()
    copy.wait()


def take_pair(kv, token):
    any_space = pl.BlockSpec(memory_space=pl.ANY)
    return pl.pallas_call(
        take_pair_kernel,
        in_specs=[any_space] * 2,
        out_specs=pl.BlockSpec(memory_space=pltpu.VMEM),
        out_shape=jax.ShapeDtypeStruct((kv.shape[0], 2 * TILE, LANES), BF16),
        scratch_shapes=[pltpu.SemaphoreType.DMA],
        name="take_pair",
    )(kv, token)


def unpack_kernel(single_ref, pair_ref, out_ref, held_ref, single_sems, pair_sems):
    groups = pair_ref.shape[0]
    first = single_ref.shape[1] - HD

    def pair_copy(g):
        target = out_ref.at[:, pl.ds((g // 2 * 3 + g % 2 * 2) * LANES, LANES)]
        return pltpu.make_async_copy(pair_ref.at[g], target, pair_sems.at[g])

    def single_copy(u):
        return pltpu.make_async_copy(held_ref.at[u], out_ref.at[:, pl.ds((3 * u + 1) * LANES, LANES)], single_sems.at[u])

    for g in range(groups):
        pair_copy(g).start()
    for u in range(groups // 2):
        both = [single_ref[2 * u + n, first:, :] for n in range(2)]
        held_ref[u] = jnp.transpose(jnp.concatenate(both, axis=0))
        single_copy(u).start()
    for g in range(groups):
        pair_copy(g).wait()
    for u in range(groups // 2):
        single_copy(u).wait()


def unpack(single, pair):
    groups = single.shape[0]
    any_space = pl.BlockSpec(memory_space=pl.ANY)
    return pl.pallas_call(
        unpack_kernel,
        in_specs=[pl.BlockSpec(memory_space=pltpu.VMEM)] * 2,
        out_specs=any_space,
        out_shape=jax.ShapeDtypeStruct((TILE, groups * 3 * HD), BF16),
        scratch_shapes=[
            pltpu.VMEM((groups // 2, TILE, LANES), BF16),
            pltpu.SemaphoreType.DMA((groups // 2,)),
            pltpu.SemaphoreType.DMA((groups,)),
        ],
        name="unpack",
    )(single, pair)


def neighbour_lists(offsets, block_mask):
    spots = jnp.arange(LAYER, dtype=jnp.int32)
    layer = lax.axis_index("seq") + offsets[None, :, 0]
    moved_h = spots[:, None] // TW + offsets[None, :, 1]
    moved_w = spots[:, None] % TW + offsets[None, :, 2]
    live = (
        (moved_h >= 0)
        & (moved_h < TH)
        & (moved_w >= 0)
        & (moved_w < TW)
        & (layer >= 0)
        & (layer < lax.axis_size("seq"))
        & (block_mask == 1)
    )
    target = ((offsets[None, :, 0] + 1) * TH + moved_h) * TW + moved_w
    ones = live.astype(jnp.int32)
    earlier = jnp.arange(NB)[:, None] < jnp.arange(NB)[None, :]
    place = jnp.sum(jnp.where(earlier[None], ones[:, :, None], 0), axis=1)
    slots = jnp.arange(SLOTS, dtype=jnp.int32)
    chosen = live[:, :, None] & (place[:, :, None] == slots[None, None, :])
    table = jnp.sum(jnp.where(chosen, target[:, :, None], 0), axis=1)
    counts = jnp.sum(ones, axis=1)
    ahead = (counts[:, None] > counts[None, :]) | ((counts[:, None] == counts[None, :]) & (spots[:, None] < spots[None, :]))
    rank = jnp.sum(ahead.astype(jnp.int32), axis=0)
    order = jnp.sum(jnp.where(rank[:, None] == spots[None, :], spots[:, None], 0), axis=0)
    return counts, order, table.reshape(-1)


def attend_rows(units, text_bias, groups, score_ref):
    tops = []
    for n, unit in enumerate(units):
        scores = unit["score"](unit["queries"], unit["text_k"]) + text_bias
        parts = [scores[:, :LANES], scores[:, LANES:]]
        score_ref[n, 0] = parts[0]
        score_ref[n, 1] = parts[1]
        tops.append(jnp.maximum(parts[0], parts[1]))
    for g in range(groups):
        for n, unit in enumerate(units):
            keys = [unit["keys"](g * GROUP + j) for j in range(GROUP)]
            found = unit["score"](unit["queries"], jnp.concatenate(keys, axis=unit["key_axis"]))
            for j in range(GROUP):
                part = found[:, j * LANES : (j + 1) * LANES]
                if unit["bias"] is not None:
                    part = part + unit["bias"](g * GROUP + j)
                score_ref[n, 2 + g * GROUP + j] = part
                tops[n] = jnp.maximum(tops[n], part)
    highest = [jnp.max(top, axis=1, keepdims=True) for top in tops]
    shifts = [top * FACTOR for top in highest]
    totals, mixed = [], []
    for n, unit in enumerate(units):
        weights = [jnp.exp2(score_ref[n, j] * FACTOR - shifts[n]) for j in range(2)]
        totals.append(weights[0] + weights[1])
        mixed.append(unit["mix"](jnp.concatenate([w.astype(BF16) for w in weights], axis=1), unit["text_v"]))
    for g in range(groups):
        for n, unit in enumerate(units):
            weights = [jnp.exp2(score_ref[n, 2 + g * GROUP + j] * FACTOR - shifts[n]) for j in range(GROUP)]
            totals[n] = totals[n] + ((weights[0] + weights[1]) + (weights[2] + weights[3]))
            values = jnp.concatenate([unit["values"](g * GROUP + j) for j in range(GROUP)], axis=unit["value_axis"])
            mixed[n] = mixed[n] + unit["mix"](jnp.concatenate([w.astype(BF16) for w in weights], axis=1), values)
    return highest, [jnp.sum(total, axis=1, keepdims=True) for total in totals], mixed


PAIR = dict(score=dot_nt, key_axis=0, mix=dot_nn, value_axis=0)
SINGLE = dict(score=dot_nn, key_axis=1, mix=dot_nt, value_axis=1)


def video_kernel(
    heads, together, query_row, own_row, counts_ref, order_ref, table_ref, q_any, before_any, own_any, after_any,
    text_k_ref, text_v_ref, bias_ref, out_ref, kv_ref, q_ref, score_ref, sems,
):
    rows = kv_ref.shape[1] // 2
    moves = [
        (before_any, kv_ref.at[pl.ds(0, LAYER)]),
        (own_any.at[:, pl.ds(own_row, 2 * rows)], kv_ref.at[pl.ds(LAYER, LAYER)]),
        (after_any, kv_ref.at[pl.ds(2 * LAYER, LAYER)]),
        (q_any.at[:, pl.ds(query_row, rows)], q_ref),
    ]
    copies = [pltpu.make_async_copy(source, target, sems.at[n]) for n, (source, target) in enumerate(moves)]
    for copy in copies:
        copy.start()
    for copy in copies:
        copy.wait()

    def unit_of(i):
        low = low_lanes(TILE)
        block = q_ref[i].astype(F32)
        if heads == 1:
            queries = jnp.transpose(block)
        else:
            queries = jnp.concatenate([jnp.where(low, block, 0.0), jnp.where(low, 0.0, block)], axis=0)
        count = counts_ref[i]
        return dict(
            SINGLE if heads == 1 else PAIR,
            queries=queries.astype(BF16),
            text_k=text_k_ref[...],
            text_v=text_v_ref[...],
            keys=lambda slot: kv_ref[table_ref[i * SLOTS + slot], :rows, :],
            values=lambda slot: kv_ref[table_ref[i * SLOTS + slot], rows:, :],
            bias=lambda slot: jnp.where(slot < count, 0.0, NEG_FILL),
        )

    def some_tiles(step, carry):
        tiles = [order_ref[step * together + n] for n in range(together)]
        longest = functools.reduce(jnp.maximum, [counts_ref[i] for i in tiles])
        for groups in range(SLOTS // GROUP + 1):

            @pl.when((longest + (GROUP - 1)) // GROUP == groups)
            def _():
                _, totals, mixed = attend_rows([unit_of(i) for i in tiles], bias_ref[...], groups, score_ref)
                for n, i in enumerate(tiles):
                    result = mixed[n] / totals[n]
                    if heads == 1:
                        out_ref[i] = jnp.transpose(result).astype(BF16)
                    else:
                        out_ref[i] = jnp.where(low_lanes(TILE), result[:TILE], result[TILE:]).astype(BF16)

        return carry

    lax.fori_loop(0, LAYER // together, some_tiles, 0)


def video_attention(heads, lists, queries, query_row, before, own, own_row, after, text_k, text_v, text_bias):
    rows = heads * HD
    together = 2
    smem = pl.BlockSpec(memory_space=pltpu.SMEM)
    vmem = pl.BlockSpec(memory_space=pltpu.VMEM)
    hbm = pl.BlockSpec(memory_space=pl.ANY)
    pairs = 300 * TILE * TILE * heads
    return pl.pallas_call(
        functools.partial(video_kernel, heads, together, query_row, own_row),
        in_specs=[smem] * 3 + [hbm] * 4 + [vmem] * 3,
        out_specs=vmem,
        out_shape=jax.ShapeDtypeStruct((LAYER, rows, LANES), BF16),
        scratch_shapes=[
            pltpu.VMEM((3 * LAYER, 2 * rows, LANES), BF16),
            pltpu.VMEM((LAYER, rows, LANES), BF16),
            pltpu.VMEM((together, 2 + SLOTS, heads * TILE, LANES), F32),
            pltpu.SemaphoreType.DMA((4,)),
        ],
        compiler_params=pltpu.CompilerParams(vmem_limit_bytes=VMEM_LIMIT),
        cost_estimate=pl.CostEstimate(flops=16 * HD * pairs, bytes_accessed=8 * before.size, transcendentals=pairs),
        name=f"video_attention_{heads}",
    )(*lists, queries, before, own, after, text_k, text_v, text_bias)


def put_text(ref, means, weighs):
    kept = ref.shape[0]
    low = low_lanes(kept)
    ref[:, :LANES] = jnp.where(low, means[0][:kept], means[1][:kept])
    lane = lax.broadcasted_iota(jnp.int32, (kept, HD), 1)
    last = jnp.zeros((kept, HD), F32)
    for head in range(3):
        last = jnp.where(lane == head, weighs[head][:kept], last)
    ref[:, LANES:] = jnp.concatenate([means[2][:kept], last], axis=1)


def merge_text(refs):
    means, weighs = [], []
    for head in range(3):
        lane = LANES + HD + head
        columns = slice(0, LANES) if head < 2 else slice(LANES, LANES + HD)
        marks = [ref[:, lane : lane + 1] for ref in refs]
        top = jnp.maximum(jnp.maximum(marks[0], marks[2]), jnp.maximum(marks[1], marks[3]))
        weights = [jnp.exp2(mark - top) for mark in marks]
        total = (weights[0] + weights[2]) + (weights[1] + weights[3])
        parts = [ref[:, columns] * (weight / total) for ref, weight in zip(refs, weights)]
        means.append((parts[0] + parts[2]) + (parts[1] + parts[3]))
        weighs.append(top + jnp.log2(total))
    return means, weighs


def merge_kernel(*refs):
    put_text(refs[4], *merge_text(refs[:4]))


def last_merge_kernel(*refs):
    means, _ = merge_text(refs[:4])
    pair_ref, single_ref = refs[4:]
    pair_ref[...] = jnp.where(low_lanes(means[0].shape[0]), means[0], means[1]).astype(BF16)
    single_ref[...] = means[2].astype(BF16)


def merge(parts, last):
    vmem = pl.BlockSpec(memory_space=pltpu.VMEM)
    rows = parts[0].shape[0]
    return pl.pallas_call(
        last_merge_kernel if last else merge_kernel,
        in_specs=[vmem] * 4,
        out_specs=[vmem] * 2 if last else vmem,
        out_shape=[jax.ShapeDtypeStruct((rows, n), BF16) for n in (LANES, HD)] if last else parts[0],
        name="text_merge",
    )(*parts)


def from_others(part, stride):
    count = lax.axis_size("seq")
    ring = 4 * stride
    parts = [part]
    for step in range(1, 4):
        pairs = [(i, i // ring * ring + (i + step * stride) % ring) for i in range(count)]
        parts.append(lax.ppermute(part, "seq", pairs))
    return parts


def text_kernel(
    kv_ref, pair_q_ref, pair_k_ref, pair_v_ref, single_q_ref, single_k_ref, single_v_ref, bias_ref,
    before_any, after_any, out_ref, score_ref,
):
    del before_any, after_any
    low = low_lanes(TEXT_ROWS)
    pair_q = pair_q_ref[...].astype(F32)

    def pair_unit(head):
        return dict(
            PAIR,
            queries=jnp.where(low if head == 0 else ~low, pair_q, 0.0).astype(BF16),
            text_k=pair_k_ref[...],
            text_v=pair_v_ref[...],
            keys=lambda slot: kv_ref[slot, 2 * HD : 2 * HD + TILE, :],
            values=lambda slot: kv_ref[slot, 2 * HD + TILE :, :],
            bias=None,
        )

    single_unit = dict(
        SINGLE,
        queries=single_q_ref[...],
        text_k=single_k_ref[...],
        text_v=single_v_ref[...],
        keys=lambda slot: kv_ref[slot, :HD, :],
        values=lambda slot: kv_ref[slot, HD : 2 * HD, :],
        bias=None,
    )
    tops, totals, mixed = attend_rows([pair_unit(0), pair_unit(1), single_unit], bias_ref[...], LAYER // GROUP, score_ref)
    means = [m / t for m, t in zip(mixed, totals)]
    weighs = [top * FACTOR + jnp.log2(total) for top, total in zip(tops, totals)]
    put_text(out_ref, means, weighs)


def text_partial(kv, pair_q, pair_k, pair_v, single_q, single_k, single_v, bias, earlier):
    vmem = pl.BlockSpec(memory_space=pltpu.VMEM)
    pairs = 3 * TEXT_ROWS * (LAYER + 2) * TILE
    return pl.pallas_call(
        text_kernel,
        in_specs=[vmem] * 8 + [pl.BlockSpec(memory_space=pl.ANY)] * len(earlier),
        out_specs=vmem,
        out_shape=jax.ShapeDtypeStruct((TEXT_KEPT, 2 * LANES), F32),
        scratch_shapes=[pltpu.VMEM((3, 2 + LAYER, TEXT_ROWS, LANES), F32)],
        compiler_params=pltpu.CompilerParams(vmem_limit_bytes=VMEM_LIMIT),
        cost_estimate=pl.CostEstimate(flops=16 * HD * pairs, bytes_accessed=4 * kv.size, transcendentals=pairs),
        name="text_partial",
    )(kv, pair_q, pair_k, pair_v, single_q, single_k, single_v, bias, *earlier)


def exchange(blocks, axis):
    return lax.all_to_all(blocks, axis, split_axis=0, concat_axis=0, tiled=True)


def both_sides(layer):
    count = lax.axis_size("seq")
    up = [(i, i + 1) for i in range(count - 1)]
    down = [(i + 1, i) for i in range(count - 1)]
    return lax.ppermute(layer, "seq", up), lax.ppermute(layer, "seq", down)


def after(value, *others):
    return lax.optimization_barrier((value,) + others)[0]


def body(video_q, video_k, video_v, text_q, text_k, text_v, offsets, block_mask, text_mask):
    odd = lax.axis_index("head") % 2 == 1

    def split_text(text):
        grown = jnp.pad(text, ((0, TEXT_ROWS - TEXT), (0, 0)))
        return jnp.where(odd, grown[:, HD:], grown[:, : 2 * HD]), jnp.where(odd, grown[:, :HD], grown[:, 2 * HD :])

    (pair_tq, single_tq), (pair_tk, single_tk), (pair_tv, single_tv) = map(split_text, (text_q, text_k, text_v))
    single_tk, single_tv = single_tk.T, single_tv.T
    text_live = jnp.pad(text_mask, (0, TEXT_ROWS - TEXT)) == 1
    bias = jnp.where(text_live, 0.0, NEG_FILL).astype(F32)[None, :]
    own_bias = jnp.where(lax.axis_index("seq") == 0, bias, NEG_FILL)

    lists = neighbour_lists(offsets, block_mask)
    text = (pair_tq, pair_tk, pair_tv, single_tq, single_tk, single_tv)
    kv = exchange(pack(video_k, video_v), "head")
    kv, queries, *rest = lax.optimization_barrier((kv, pack(video_q)) + lists + text)
    lists, (pair_tq, pair_tk, pair_tv, single_tq, single_tk, single_tv) = rest[:3], rest[3:]
    queries = exchange(after(queries, kv), "head")
    single_before, single_after = both_sides(kv[:, : 2 * HD])
    token, _ = both_sides(kv[0, :16])
    pair_before, pair_after = both_sides(take_pair(kv, token))
    partial = text_partial(kv, pair_tq, pair_tk, pair_tv, single_tq, single_tk, single_tv, own_bias, (single_before, single_after))
    partial = from_others(partial, 4)

    single_out = video_attention(
        1, lists, queries, 0, single_before, kv, 0, single_after, single_tk, single_tv, bias
    )
    *partial, single_out = lax.optimization_barrier((*partial, single_out))
    single_back = exchange(single_out, "head")
    partial = from_others(merge(partial, False), 1)
    pair_q = after(queries, single_out)
    pair_out = video_attention(2, lists, pair_q, HD, pair_before, kv, 2 * HD, pair_after, pair_tk, pair_tv, bias)
    pair_back = exchange(after(pair_out, single_back, *partial), "head")
    video_out = unpack(single_back, pair_back)

    pair_part, single_part = (part[:TEXT] for part in merge(partial, True))
    text_out = jnp.where(
        odd,
        jnp.concatenate([single_part, pair_part], axis=1),
        jnp.concatenate([pair_part, single_part], axis=1),
    )
    return video_out, text_out


def solution(mesh):
    return jax.shard_map(
        body,
        mesh=mesh,
        in_specs=(
            P(("seq", "head"), None),
            P(("seq", "head"), None),
            P(("seq", "head"), None),
            P(None, "head"),
            P(None, "head"),
            P(None, "head"),
            P(),
            P("seq", None),
            P(),
        ),
        out_specs=(P(("seq", "head"), None), P(None, "head")),
        check_vma=False,
    )
```

```python
import functools
import math

import jax
import jax.numpy as jnp
from jax import lax
from jax.experimental import pallas as pl
from jax.experimental.pallas import tpu as pltpu
from jax.sharding import PartitionSpec as P

HD = 64
TEXT = 226
TEXT_ROWS = 256
TEXT_KEPT = 232
TILE = 128
TH = 4
TW = 4
LAYER = TH * TW
NB = 27
GROUP = 4
SLOTS = 28
LANES = 128
NEG_FILL = -jnp.inf
FACTOR = math.log2(math.e) / math.sqrt(HD)
BF16 = jnp.bfloat16
F32 = jnp.float32
VMEM_LIMIT = 56 * 1024 * 1024


def low_lanes(rows):
    return lax.broadcasted_iota(jnp.int32, (rows, LANES), 1) < HD


def dot_nt(a, b):
    return lax.dot_general(a, b, (((1,), (1,)), ((), ())), preferred_element_type=F32)


def dot_nn(a, b):
    return lax.dot_general(a, b, (((1,), (0,)), ((), ())), preferred_element_type=F32)


def pack_kernel(*refs):
    count = len(refs) - 3
    arrays, (out_ref, held_ref, sems) = refs[:count], refs[count:]
    groups = out_ref.shape[0]

    def single_copy(n, u):
        source = arrays[n].at[:, pl.ds((3 * u + 1) * LANES, LANES)]
        return pltpu.make_async_copy(source, held_ref.at[n, u], sems.at[n, groups + u])

    def pair_copy(n, g):
        source = arrays[n].at[:, pl.ds((g // 2 * 3 + g % 2 * 2) * LANES, LANES)]
        return pltpu.make_async_copy(source, out_ref.at[g, pl.ds(count * HD + n * TILE, TILE)], sems.at[n, g])

    singles = [(n, u) for u in range(groups // 2) for n in range(count)]
    pairs = [(n, g) for g in range(groups) for n in range(count)]
    for n, u in singles:
        single_copy(n, u).start()
    for n, g in pairs:
        pair_copy(n, g).start()
    for n, u in singles:
        single_copy(n, u).wait()
        turned = jnp.transpose(held_ref[n, u])
        out_ref[2 * u, n * HD : (n + 1) * HD, :] = turned[:HD]
        out_ref[2 * u + 1, n * HD : (n + 1) * HD, :] = turned[HD:]
    for n, g in pairs:
        pair_copy(n, g).wait()


def pack(*arrays):
    count = len(arrays)
    groups = arrays[0].shape[1] // (3 * HD)
    return pl.pallas_call(
        pack_kernel,
        in_specs=[pl.BlockSpec(memory_space=pl.ANY)] * count,
        out_specs=pl.BlockSpec(memory_space=pltpu.VMEM),
        out_shape=jax.ShapeDtypeStruct((groups, count * 3 * HD, LANES), BF16),
        scratch_shapes=[
            pltpu.VMEM((count, groups // 2, TILE, LANES), BF16),
            pltpu.SemaphoreType.DMA((count, groups + groups // 2)),
        ],
        cost_estimate=pl.CostEstimate(flops=0, bytes_accessed=4 * count * arrays[0].size, transcendentals=0),
        name="pack",
    )(*arrays)


def unpack_kernel(single_ref, pair_ref, out_ref, held_ref, single_sems, pair_sems):
    groups = pair_ref.shape[0]
    first = single_ref.shape[1] - HD

    def pair_copy(g):
        target = out_ref.at[:, pl.ds((g // 2 * 3 + g % 2 * 2) * LANES, LANES)]
        return pltpu.make_async_copy(pair_ref.at[g], target, pair_sems.at[g])

    def single_copy(u):
        return pltpu.make_async_copy(held_ref.at[u], out_ref.at[:, pl.ds((3 * u + 1) * LANES, LANES)], single_sems.at[u])

    for g in range(groups):
        pair_copy(g).start()
    for u in range(groups // 2):
        both = [single_ref[2 * u + n, first:, :] for n in range(2)]
        held_ref[u] = jnp.transpose(jnp.concatenate(both, axis=0))
        single_copy(u).start()
    for g in range(groups):
        pair_copy(g).wait()
    for u in range(groups // 2):
        single_copy(u).wait()


def unpack(single, pair):
    groups = single.shape[0]
    any_space = pl.BlockSpec(memory_space=pl.ANY)
    return pl.pallas_call(
        unpack_kernel,
        in_specs=[pl.BlockSpec(memory_space=pltpu.VMEM)] * 2,
        out_specs=any_space,
        out_shape=jax.ShapeDtypeStruct((TILE, groups * 3 * HD), BF16),
        scratch_shapes=[
            pltpu.VMEM((groups // 2, TILE, LANES), BF16),
            pltpu.SemaphoreType.DMA((groups // 2,)),
            pltpu.SemaphoreType.DMA((groups,)),
        ],
        name="unpack",
    )(single, pair)


def neighbour_lists(offsets, block_mask):
    spots = jnp.arange(LAYER, dtype=jnp.int32)
    layer = lax.axis_index("seq") + offsets[None, :, 0]
    moved_h = spots[:, None] // TW + offsets[None, :, 1]
    moved_w = spots[:, None] % TW + offsets[None, :, 2]
    live = (
        (moved_h >= 0)
        & (moved_h < TH)
        & (moved_w >= 0)
        & (moved_w < TW)
        & (layer >= 0)
        & (layer < lax.axis_size("seq"))
        & (block_mask == 1)
    )
    target = ((offsets[None, :, 0] + 1) * TH + moved_h) * TW + moved_w
    ones = live.astype(jnp.int32)
    earlier = jnp.arange(NB)[:, None] < jnp.arange(NB)[None, :]
    place = jnp.sum(jnp.where(earlier[None], ones[:, :, None], 0), axis=1)
    slots = jnp.arange(SLOTS, dtype=jnp.int32)
    chosen = live[:, :, None] & (place[:, :, None] == slots[None, None, :])
    table = jnp.sum(jnp.where(chosen, target[:, :, None], 0), axis=1)
    counts = jnp.sum(ones, axis=1)
    ahead = (counts[:, None] > counts[None, :]) | ((counts[:, None] == counts[None, :]) & (spots[:, None] < spots[None, :]))
    rank = jnp.sum(ahead.astype(jnp.int32), axis=0)
    order = jnp.sum(jnp.where(rank[:, None] == spots[None, :], spots[:, None], 0), axis=0)
    return counts, order, table.reshape(-1)


def attend_rows(units, text_bias, groups, score_ref):
    tops = []
    for n, unit in enumerate(units):
        scores = unit["score"](unit["queries"], unit["text_k"]) + text_bias
        parts = [scores[:, :LANES], scores[:, LANES:]]
        score_ref[n, 0] = parts[0]
        score_ref[n, 1] = parts[1]
        tops.append(jnp.maximum(parts[0], parts[1]))
    for g in range(groups):
        for n, unit in enumerate(units):
            keys = [unit["keys"](g * GROUP + j) for j in range(GROUP)]
            found = unit["score"](unit["queries"], jnp.concatenate(keys, axis=unit["key_axis"]))
            for j in range(GROUP):
                part = found[:, j * LANES : (j + 1) * LANES]
                if unit["bias"] is not None:
                    part = part + unit["bias"](g * GROUP + j)
                score_ref[n, 2 + g * GROUP + j] = part
                tops[n] = jnp.maximum(tops[n], part)
    highest = [jnp.max(top, axis=1, keepdims=True) for top in tops]
    shifts = [top * FACTOR for top in highest]
    totals, mixed = [], []
    for n, unit in enumerate(units):
        weights = [jnp.exp2(score_ref[n, j] * FACTOR - shifts[n]) for j in range(2)]
        totals.append(weights[0] + weights[1])
        mixed.append(unit["mix"](jnp.concatenate([w.astype(BF16) for w in weights], axis=1), unit["text_v"]))
    for g in range(groups):
        for n, unit in enumerate(units):
            weights = [jnp.exp2(score_ref[n, 2 + g * GROUP + j] * FACTOR - shifts[n]) for j in range(GROUP)]
            totals[n] = totals[n] + ((weights[0] + weights[1]) + (weights[2] + weights[3]))
            values = jnp.concatenate([unit["values"](g * GROUP + j) for j in range(GROUP)], axis=unit["value_axis"])
            mixed[n] = mixed[n] + unit["mix"](jnp.concatenate([w.astype(BF16) for w in weights], axis=1), values)
    return highest, [jnp.sum(total, axis=1, keepdims=True) for total in totals], mixed


PAIR = dict(score=dot_nt, key_axis=0, mix=dot_nn, value_axis=0)
SINGLE = dict(score=dot_nn, key_axis=1, mix=dot_nt, value_axis=1)


def video_kernel(
    heads, together, query_row, own_row, counts_ref, order_ref, table_ref, q_any, before_any, own_any, after_any,
    text_k_ref, text_v_ref, bias_ref, out_ref, kv_ref, q_ref, score_ref, sems,
):
    rows = kv_ref.shape[1] // 2
    moves = [
        (before_any, kv_ref.at[pl.ds(0, LAYER)]),
        (own_any.at[:, pl.ds(own_row, 2 * rows)], kv_ref.at[pl.ds(LAYER, LAYER)]),
        (after_any, kv_ref.at[pl.ds(2 * LAYER, LAYER)]),
        (q_any.at[:, pl.ds(query_row, rows)], q_ref),
    ]
    copies = [pltpu.make_async_copy(source, target, sems.at[n]) for n, (source, target) in enumerate(moves)]
    for copy in copies:
        copy.start()
    for copy in copies:
        copy.wait()

    def unit_of(i):
        low = low_lanes(TILE)
        block = q_ref[i].astype(F32)
        if heads == 1:
            queries = jnp.transpose(block)
        else:
            queries = jnp.concatenate([jnp.where(low, block, 0.0), jnp.where(low, 0.0, block)], axis=0)
        count = counts_ref[i]
        return dict(
            SINGLE if heads == 1 else PAIR,
            queries=queries.astype(BF16),
            text_k=text_k_ref[...],
            text_v=text_v_ref[...],
            keys=lambda slot: kv_ref[table_ref[i * SLOTS + slot], :rows, :],
            values=lambda slot: kv_ref[table_ref[i * SLOTS + slot], rows:, :],
            bias=lambda slot: jnp.where(slot < count, 0.0, NEG_FILL),
        )

    def some_tiles(step, carry):
        tiles = [order_ref[step * together + n] for n in range(together)]
        longest = functools.reduce(jnp.maximum, [counts_ref[i] for i in tiles])
        for groups in range(SLOTS // GROUP + 1):

            @pl.when((longest + (GROUP - 1)) // GROUP == groups)
            def _():
                _, totals, mixed = attend_rows([unit_of(i) for i in tiles], bias_ref[...], groups, score_ref)
                for n, i in enumerate(tiles):
                    result = mixed[n] / totals[n]
                    if heads == 1:
                        out_ref[i] = jnp.transpose(result).astype(BF16)
                    else:
                        out_ref[i] = jnp.where(low_lanes(TILE), result[:TILE], result[TILE:]).astype(BF16)

        return carry

    lax.fori_loop(0, LAYER // together, some_tiles, 0)


def video_attention(heads, lists, queries, query_row, before, own, own_row, after, text_k, text_v, text_bias):
    rows = heads * HD
    together = 2
    smem = pl.BlockSpec(memory_space=pltpu.SMEM)
    vmem = pl.BlockSpec(memory_space=pltpu.VMEM)
    hbm = pl.BlockSpec(memory_space=pl.ANY)
    pairs = 300 * TILE * TILE * heads
    return pl.pallas_call(
        functools.partial(video_kernel, heads, together, query_row, own_row),
        in_specs=[smem] * 3 + [hbm] * 4 + [vmem] * 3,
        out_specs=vmem,
        out_shape=jax.ShapeDtypeStruct((LAYER, rows, LANES), BF16),
        scratch_shapes=[
            pltpu.VMEM((3 * LAYER, 2 * rows, LANES), BF16),
            pltpu.VMEM((LAYER, rows, LANES), BF16),
            pltpu.VMEM((together, 2 + SLOTS, heads * TILE, LANES), F32),
            pltpu.SemaphoreType.DMA((4,)),
        ],
        compiler_params=pltpu.CompilerParams(vmem_limit_bytes=VMEM_LIMIT),
        cost_estimate=pl.CostEstimate(flops=16 * HD * pairs, bytes_accessed=8 * before.size, transcendentals=pairs),
        name=f"video_attention_{heads}",
    )(*lists, queries, before, own, after, text_k, text_v, text_bias)


def put_text(ref, means, weighs):
    kept = ref.shape[0]
    low = low_lanes(kept)
    ref[:, :LANES] = jnp.where(low, means[0][:kept], means[1][:kept])
    lane = lax.broadcasted_iota(jnp.int32, (kept, HD), 1)
    last = jnp.zeros((kept, HD), F32)
    for head in range(3):
        last = jnp.where(lane == head, weighs[head][:kept], last)
    ref[:, LANES:] = jnp.concatenate([means[2][:kept], last], axis=1)


def merge_text(refs):
    means, weighs = [], []
    for head in range(3):
        lane = LANES + HD + head
        columns = slice(0, LANES) if head < 2 else slice(LANES, LANES + HD)
        marks = [ref[:, lane : lane + 1] for ref in refs]
        top = jnp.maximum(jnp.maximum(marks[0], marks[2]), jnp.maximum(marks[1], marks[3]))
        weights = [jnp.exp2(mark - top) for mark in marks]
        total = (weights[0] + weights[2]) + (weights[1] + weights[3])
        parts = [ref[:, columns] * (weight / total) for ref, weight in zip(refs, weights)]
        means.append((parts[0] + parts[2]) + (parts[1] + parts[3]))
        weighs.append(top + jnp.log2(total))
    return means, weighs


def merge_kernel(*refs):
    put_text(refs[4], *merge_text(refs[:4]))


def last_merge_kernel(*refs):
    means, _ = merge_text(refs[:4])
    pair_ref, single_ref = refs[4:]
    pair_ref[...] = jnp.where(low_lanes(means[0].shape[0]), means[0], means[1]).astype(BF16)
    single_ref[...] = means[2].astype(BF16)


def merge(parts, last):
    vmem = pl.BlockSpec(memory_space=pltpu.VMEM)
    rows = parts[0].shape[0]
    return pl.pallas_call(
        last_merge_kernel if last else merge_kernel,
        in_specs=[vmem] * 4,
        out_specs=[vmem] * 2 if last else vmem,
        out_shape=[jax.ShapeDtypeStruct((rows, n), BF16) for n in (LANES, HD)] if last else parts[0],
        name="text_merge",
    )(*parts)


def from_others(part, stride):
    count = lax.axis_size("seq")
    ring = 4 * stride
    parts = [part]
    for step in range(1, 4):
        pairs = [(i, i // ring * ring + (i + step * stride) % ring) for i in range(count)]
        parts.append(lax.ppermute(part, "seq", pairs))
    return parts


def text_kernel(
    kv_ref, pair_q_ref, pair_k_ref, pair_v_ref, single_q_ref, single_k_ref, single_v_ref, bias_ref,
    earlier_ref, out_ref, score_ref,
):
    del earlier_ref
    low = low_lanes(TEXT_ROWS)
    pair_q = pair_q_ref[...].astype(F32)

    def pair_unit(head):
        return dict(
            PAIR,
            queries=jnp.where(low if head == 0 else ~low, pair_q, 0.0).astype(BF16),
            text_k=pair_k_ref[...],
            text_v=pair_v_ref[...],
            keys=lambda slot: kv_ref[slot, 2 * HD : 2 * HD + TILE, :],
            values=lambda slot: kv_ref[slot, 2 * HD + TILE :, :],
            bias=None,
        )

    single_unit = dict(
        SINGLE,
        queries=single_q_ref[...],
        text_k=single_k_ref[...],
        text_v=single_v_ref[...],
        keys=lambda slot: kv_ref[slot, :HD, :],
        values=lambda slot: kv_ref[slot, HD : 2 * HD, :],
        bias=None,
    )
    tops, totals, mixed = attend_rows([pair_unit(0), pair_unit(1), single_unit], bias_ref[...], LAYER // GROUP, score_ref)
    means = [m / t for m, t in zip(mixed, totals)]
    weighs = [top * FACTOR + jnp.log2(total) for top, total in zip(tops, totals)]
    put_text(out_ref, means, weighs)


def text_partial(kv, pair_q, pair_k, pair_v, single_q, single_k, single_v, bias, earlier):
    vmem = pl.BlockSpec(memory_space=pltpu.VMEM)
    pairs = 3 * TEXT_ROWS * (LAYER + 2) * TILE
    return pl.pallas_call(
        text_kernel,
        in_specs=[vmem] * 8 + [pl.BlockSpec(memory_space=pl.ANY)],
        out_specs=vmem,
        out_shape=jax.ShapeDtypeStruct((TEXT_KEPT, 2 * LANES), F32),
        scratch_shapes=[pltpu.VMEM((3, 2 + LAYER, TEXT_ROWS, LANES), F32)],
        compiler_params=pltpu.CompilerParams(vmem_limit_bytes=VMEM_LIMIT),
        cost_estimate=pl.CostEstimate(flops=16 * HD * pairs, bytes_accessed=4 * kv.size, transcendentals=pairs),
        name="text_partial",
    )(kv, pair_q, pair_k, pair_v, single_q, single_k, single_v, bias, earlier)


def exchange(blocks, axis):
    return lax.all_to_all(blocks, axis, split_axis=0, concat_axis=0, tiled=True)


def both_sides(layer):
    count = lax.axis_size("seq")
    up = [(i, i + 1) for i in range(count - 1)]
    down = [(i + 1, i) for i in range(count - 1)]
    return lax.ppermute(layer, "seq", up), lax.ppermute(layer, "seq", down)


def after(value, *others):
    return lax.optimization_barrier((value,) + others)[0]


def body(video_q, video_k, video_v, text_q, text_k, text_v, offsets, block_mask, text_mask):
    odd = lax.axis_index("head") % 2 == 1

    def split_text(text):
        grown = jnp.pad(text, ((0, TEXT_ROWS - TEXT), (0, 0)))
        return jnp.where(odd, grown[:, HD:], grown[:, : 2 * HD]), jnp.where(odd, grown[:, :HD], grown[:, 2 * HD :])

    (pair_tq, single_tq), (pair_tk, single_tk), (pair_tv, single_tv) = map(split_text, (text_q, text_k, text_v))
    single_tk, single_tv = single_tk.T, single_tv.T
    text_live = jnp.pad(text_mask, (0, TEXT_ROWS - TEXT)) == 1
    bias = jnp.where(text_live, 0.0, NEG_FILL).astype(F32)[None, :]
    own_bias = jnp.where(lax.axis_index("seq") == 0, bias, NEG_FILL)

    lists = neighbour_lists(offsets, block_mask)
    text = (pair_tq, pair_tk, pair_tv, single_tq, single_tk, single_tv)
    kv = exchange(pack(video_k, video_v), "head")
    kv, queries, *rest = lax.optimization_barrier((kv, pack(video_q)) + lists + text)
    lists, (pair_tq, pair_tk, pair_tv, single_tq, single_tk, single_tv) = rest[:3], rest[3:]
    queries = exchange(after(queries, kv), "head")
    single_kv = kv[:, : 2 * HD]
    single_before, single_after = both_sides(single_kv)
    token, _ = both_sides(kv[0, :16])
    pair_before, pair_after = both_sides(kv[:, 2 * HD :])
    partial = text_partial(kv, pair_tq, pair_tk, pair_tv, single_tq, single_tk, single_tv, own_bias, token)
    partial = from_others(partial, 4)

    partial = merge(partial, False)
    pair_q = after(queries, partial)
    partial = from_others(partial, 1)

    pair_out = video_attention(2, lists, pair_q, HD, pair_before, kv, 2 * HD, pair_after, pair_tk, pair_tv, bias)
    pair_back = exchange(pair_out, "head")
    single_q = after(queries, pair_out)
    single_out = video_attention(
        1, lists, single_q, 0, single_before, kv, 0, single_after, single_tk, single_tv, bias
    )
    single_back = exchange(after(single_out, pair_back, *partial), "head")
    video_out = unpack(single_back, pair_back)

    pair_part, single_part = (part[:TEXT] for part in merge(partial, True))
    text_out = jnp.where(
        odd,
        jnp.concatenate([single_part, pair_part], axis=1),
        jnp.concatenate([pair_part, single_part], axis=1),
    )
    return video_out, text_out


def solution(mesh):
    return jax.shard_map(
        body,
        mesh=mesh,
        in_specs=(
            P(("seq", "head"), None),
            P(("seq", "head"), None),
            P(("seq", "head"), None),
            P(None, "head"),
            P(None, "head"),
            P(None, "head"),
            P(),
            P("seq", None),
            P(),
        ),
        out_specs=(P(("seq", "head"), None), P(None, "head")),
        check_vma=False,
    )
```

```python
import functools
import math

import jax
import jax.numpy as jnp
from jax import lax
from jax.experimental import pallas as pl
from jax.experimental.pallas import tpu as pltpu
from jax.sharding import PartitionSpec as P

HD = 64
TEXT = 226
TEXT_ROWS = 256
TEXT_KEPT = 232
TILE = 128
TH = 4
TW = 4
LAYER = TH * TW
NB = 27
GROUP = 4
SLOTS = 28
LANES = 128
NEG_FILL = -jnp.inf
FACTOR = math.log2(math.e) / math.sqrt(HD)
BF16 = jnp.bfloat16
F32 = jnp.float32
VMEM_LIMIT = 56 * 1024 * 1024


def low_lanes(rows):
    return lax.broadcasted_iota(jnp.int32, (rows, LANES), 1) < HD


def dot_nt(a, b):
    return lax.dot_general(a, b, (((1,), (1,)), ((), ())), preferred_element_type=F32)


def dot_nn(a, b):
    return lax.dot_general(a, b, (((1,), (0,)), ((), ())), preferred_element_type=F32)


def pack_kernel(*refs):
    count = len(refs) - 3
    arrays, (out_ref, held_ref, sems) = refs[:count], refs[count:]
    groups = out_ref.shape[0]

    def single_copy(n, u):
        source = arrays[n].at[:, pl.ds((3 * u + 1) * LANES, LANES)]
        return pltpu.make_async_copy(source, held_ref.at[n, u], sems.at[n, groups + u])

    def pair_copy(n, g):
        source = arrays[n].at[:, pl.ds((g // 2 * 3 + g % 2 * 2) * LANES, LANES)]
        return pltpu.make_async_copy(source, out_ref.at[g, pl.ds(count * HD + n * TILE, TILE)], sems.at[n, g])

    singles = [(n, u) for u in range(groups // 2) for n in range(count)]
    pairs = [(n, g) for g in range(groups) for n in range(count)]
    for n, u in singles:
        single_copy(n, u).start()
    for n, g in pairs:
        pair_copy(n, g).start()
    for n, u in singles:
        single_copy(n, u).wait()
        turned = jnp.transpose(held_ref[n, u])
        out_ref[2 * u, n * HD : (n + 1) * HD, :] = turned[:HD]
        out_ref[2 * u + 1, n * HD : (n + 1) * HD, :] = turned[HD:]
    for n, g in pairs:
        pair_copy(n, g).wait()


def pack(*arrays):
    count = len(arrays)
    groups = arrays[0].shape[1] // (3 * HD)
    return pl.pallas_call(
        pack_kernel,
        in_specs=[pl.BlockSpec(memory_space=pl.ANY)] * count,
        out_specs=pl.BlockSpec(memory_space=pltpu.VMEM),
        out_shape=jax.ShapeDtypeStruct((groups, count * 3 * HD, LANES), BF16),
        scratch_shapes=[
            pltpu.VMEM((count, groups // 2, TILE, LANES), BF16),
            pltpu.SemaphoreType.DMA((count, groups + groups // 2)),
        ],
        cost_estimate=pl.CostEstimate(flops=0, bytes_accessed=4 * count * arrays[0].size, transcendentals=0),
        name="pack",
    )(*arrays)


def unpack_kernel(single_ref, pair_ref, out_ref, held_ref, single_sems, pair_sems):
    groups = pair_ref.shape[0]
    first = single_ref.shape[1] - HD

    def pair_copy(g):
        target = out_ref.at[:, pl.ds((g // 2 * 3 + g % 2 * 2) * LANES, LANES)]
        return pltpu.make_async_copy(pair_ref.at[g], target, pair_sems.at[g])

    def single_copy(u):
        return pltpu.make_async_copy(held_ref.at[u], out_ref.at[:, pl.ds((3 * u + 1) * LANES, LANES)], single_sems.at[u])

    for g in range(groups):
        pair_copy(g).start()
    for u in range(groups // 2):
        both = [single_ref[2 * u + n, first:, :] for n in range(2)]
        held_ref[u] = jnp.transpose(jnp.concatenate(both, axis=0))
        single_copy(u).start()
    for g in range(groups):
        pair_copy(g).wait()
    for u in range(groups // 2):
        single_copy(u).wait()


def unpack(single, pair):
    groups = single.shape[0]
    any_space = pl.BlockSpec(memory_space=pl.ANY)
    return pl.pallas_call(
        unpack_kernel,
        in_specs=[pl.BlockSpec(memory_space=pltpu.VMEM)] * 2,
        out_specs=any_space,
        out_shape=jax.ShapeDtypeStruct((TILE, groups * 3 * HD), BF16),
        scratch_shapes=[
            pltpu.VMEM((groups // 2, TILE, LANES), BF16),
            pltpu.SemaphoreType.DMA((groups // 2,)),
            pltpu.SemaphoreType.DMA((groups,)),
        ],
        name="unpack",
    )(single, pair)


def neighbour_lists(offsets, block_mask):
    spots = jnp.arange(LAYER, dtype=jnp.int32)
    layer = lax.axis_index("seq") + offsets[None, :, 0]
    moved_h = spots[:, None] // TW + offsets[None, :, 1]
    moved_w = spots[:, None] % TW + offsets[None, :, 2]
    live = (
        (moved_h >= 0)
        & (moved_h < TH)
        & (moved_w >= 0)
        & (moved_w < TW)
        & (layer >= 0)
        & (layer < lax.axis_size("seq"))
        & (block_mask == 1)
    )
    target = ((offsets[None, :, 0] + 1) * TH + moved_h) * TW + moved_w
    ones = live.astype(jnp.int32)
    earlier = jnp.arange(NB)[:, None] < jnp.arange(NB)[None, :]
    place = jnp.sum(jnp.where(earlier[None], ones[:, :, None], 0), axis=1)
    slots = jnp.arange(SLOTS, dtype=jnp.int32)
    chosen = live[:, :, None] & (place[:, :, None] == slots[None, None, :])
    table = jnp.sum(jnp.where(chosen, target[:, :, None], 0), axis=1)
    counts = jnp.sum(ones, axis=1)
    ahead = (counts[:, None] > counts[None, :]) | ((counts[:, None] == counts[None, :]) & (spots[:, None] < spots[None, :]))
    rank = jnp.sum(ahead.astype(jnp.int32), axis=0)
    order = jnp.sum(jnp.where(rank[:, None] == spots[None, :], spots[:, None], 0), axis=0)
    return counts, order, table.reshape(-1)


def attend_rows(units, text_bias, groups, score_ref):
    tops = []
    for n, unit in enumerate(units):
        scores = unit["score"](unit["queries"], unit["text_k"]) + text_bias
        parts = [scores[:, :LANES], scores[:, LANES:]]
        score_ref[n, 0] = parts[0]
        score_ref[n, 1] = parts[1]
        tops.append(jnp.maximum(parts[0], parts[1]))
    for g in range(groups):
        for n, unit in enumerate(units):
            keys = [unit["keys"](g * GROUP + j) for j in range(GROUP)]
            found = unit["score"](unit["queries"], jnp.concatenate(keys, axis=unit["key_axis"]))
            for j in range(GROUP):
                part = found[:, j * LANES : (j + 1) * LANES]
                if unit["bias"] is not None:
                    part = part + unit["bias"](g * GROUP + j)
                score_ref[n, 2 + g * GROUP + j] = part
                tops[n] = jnp.maximum(tops[n], part)
    highest = [jnp.max(top, axis=1, keepdims=True) for top in tops]
    shifts = [top * FACTOR for top in highest]
    totals, mixed = [], []
    for n, unit in enumerate(units):
        weights = [jnp.exp2(score_ref[n, j] * FACTOR - shifts[n]) for j in range(2)]
        totals.append(weights[0] + weights[1])
        mixed.append(unit["mix"](jnp.concatenate([w.astype(BF16) for w in weights], axis=1), unit["text_v"]))
    for g in range(groups):
        for n, unit in enumerate(units):
            weights = [jnp.exp2(score_ref[n, 2 + g * GROUP + j] * FACTOR - shifts[n]) for j in range(GROUP)]
            totals[n] = totals[n] + ((weights[0] + weights[1]) + (weights[2] + weights[3]))
            values = jnp.concatenate([unit["values"](g * GROUP + j) for j in range(GROUP)], axis=unit["value_axis"])
            mixed[n] = mixed[n] + unit["mix"](jnp.concatenate([w.astype(BF16) for w in weights], axis=1), values)
    return highest, [jnp.sum(total, axis=1, keepdims=True) for total in totals], mixed


PAIR = dict(score=dot_nt, key_axis=0, mix=dot_nn, value_axis=0)
SINGLE = dict(score=dot_nn, key_axis=1, mix=dot_nt, value_axis=1)


def video_kernel(
    heads, together, query_row, own_row, counts_ref, order_ref, table_ref, q_any, before_any, own_any, after_any,
    text_k_ref, text_v_ref, bias_ref, out_ref, kv_ref, q_ref, score_ref, sems,
):
    rows = kv_ref.shape[1] // 2
    moves = [
        (before_any, kv_ref.at[pl.ds(0, LAYER)]),
        (own_any.at[:, pl.ds(own_row, 2 * rows)], kv_ref.at[pl.ds(LAYER, LAYER)]),
        (after_any, kv_ref.at[pl.ds(2 * LAYER, LAYER)]),
        (q_any.at[:, pl.ds(query_row, rows)], q_ref),
    ]
    copies = [pltpu.make_async_copy(source, target, sems.at[n]) for n, (source, target) in enumerate(moves)]
    for copy in copies:
        copy.start()
    for copy in copies:
        copy.wait()

    def unit_of(i):
        low = low_lanes(TILE)
        block = q_ref[i].astype(F32)
        if heads == 1:
            queries = jnp.transpose(block)
        else:
            queries = jnp.concatenate([jnp.where(low, block, 0.0), jnp.where(low, 0.0, block)], axis=0)
        count = counts_ref[i]
        return dict(
            SINGLE if heads == 1 else PAIR,
            queries=queries.astype(BF16),
            text_k=text_k_ref[...],
            text_v=text_v_ref[...],
            keys=lambda slot: kv_ref[table_ref[i * SLOTS + slot], :rows, :],
            values=lambda slot: kv_ref[table_ref[i * SLOTS + slot], rows:, :],
            bias=lambda slot: jnp.where(slot < count, 0.0, NEG_FILL),
        )

    def some_tiles(step, carry):
        tiles = [order_ref[step * together + n] for n in range(together)]
        longest = functools.reduce(jnp.maximum, [counts_ref[i] for i in tiles])
        for groups in range(SLOTS // GROUP + 1):

            @pl.when((longest + (GROUP - 1)) // GROUP == groups)
            def _():
                _, totals, mixed = attend_rows([unit_of(i) for i in tiles], bias_ref[...], groups, score_ref)
                for n, i in enumerate(tiles):
                    result = mixed[n] / totals[n]
                    if heads == 1:
                        out_ref[i] = jnp.transpose(result).astype(BF16)
                    else:
                        out_ref[i] = jnp.where(low_lanes(TILE), result[:TILE], result[TILE:]).astype(BF16)

        return carry

    lax.fori_loop(0, LAYER // together, some_tiles, 0)


def video_attention(heads, lists, queries, query_row, before, own, own_row, after, text_k, text_v, text_bias):
    rows = heads * HD
    together = 2
    smem = pl.BlockSpec(memory_space=pltpu.SMEM)
    vmem = pl.BlockSpec(memory_space=pltpu.VMEM)
    hbm = pl.BlockSpec(memory_space=pl.ANY)
    pairs = 300 * TILE * TILE * heads
    return pl.pallas_call(
        functools.partial(video_kernel, heads, together, query_row, own_row),
        in_specs=[smem] * 3 + [hbm] * 4 + [vmem] * 3,
        out_specs=vmem,
        out_shape=jax.ShapeDtypeStruct((LAYER, rows, LANES), BF16),
        scratch_shapes=[
            pltpu.VMEM((3 * LAYER, 2 * rows, LANES), BF16),
            pltpu.VMEM((LAYER, rows, LANES), BF16),
            pltpu.VMEM((together, 2 + SLOTS, heads * TILE, LANES), F32),
            pltpu.SemaphoreType.DMA((4,)),
        ],
        compiler_params=pltpu.CompilerParams(vmem_limit_bytes=VMEM_LIMIT),
        cost_estimate=pl.CostEstimate(flops=16 * HD * pairs, bytes_accessed=8 * before.size, transcendentals=pairs),
        name=f"video_attention_{heads}",
    )(*lists, queries, before, own, after, text_k, text_v, text_bias)


def put_text(ref, means, weighs):
    kept = ref.shape[0]
    low = low_lanes(kept)
    ref[:, :LANES] = jnp.where(low, means[0][:kept], means[1][:kept])
    lane = lax.broadcasted_iota(jnp.int32, (kept, HD), 1)
    last = jnp.zeros((kept, HD), F32)
    for head in range(3):
        last = jnp.where(lane == head, weighs[head][:kept], last)
    ref[:, LANES:] = jnp.concatenate([means[2][:kept], last], axis=1)


def merge_text(refs):
    means, weighs = [], []
    for head in range(3):
        lane = LANES + HD + head
        columns = slice(0, LANES) if head < 2 else slice(LANES, LANES + HD)
        marks = [ref[:, lane : lane + 1] for ref in refs]
        top = jnp.maximum(jnp.maximum(marks[0], marks[2]), jnp.maximum(marks[1], marks[3]))
        weights = [jnp.exp2(mark - top) for mark in marks]
        total = (weights[0] + weights[2]) + (weights[1] + weights[3])
        parts = [ref[:, columns] * (weight / total) for ref, weight in zip(refs, weights)]
        means.append((parts[0] + parts[2]) + (parts[1] + parts[3]))
        weighs.append(top + jnp.log2(total))
    return means, weighs


def merge_kernel(*refs):
    put_text(refs[4], *merge_text(refs[:4]))


def last_merge_kernel(*refs):
    means, _ = merge_text(refs[:4])
    pair_ref, single_ref = refs[4:]
    pair_ref[...] = jnp.where(low_lanes(means[0].shape[0]), means[0], means[1]).astype(BF16)
    single_ref[...] = means[2].astype(BF16)


def merge(parts, last):
    vmem = pl.BlockSpec(memory_space=pltpu.VMEM)
    rows = parts[0].shape[0]
    return pl.pallas_call(
        last_merge_kernel if last else merge_kernel,
        in_specs=[vmem] * 4,
        out_specs=[vmem] * 2 if last else vmem,
        out_shape=[jax.ShapeDtypeStruct((rows, n), BF16) for n in (LANES, HD)] if last else parts[0],
        name="text_merge",
    )(*parts)


def from_others(part, stride):
    count = lax.axis_size("seq")
    ring = 4 * stride
    parts = [part]
    for step in range(1, 4):
        pairs = [(i, i // ring * ring + (i + step * stride) % ring) for i in range(count)]
        parts.append(lax.ppermute(part, "seq", pairs))
    return parts


def text_kernel(
    kv_ref, pair_q_ref, pair_k_ref, pair_v_ref, single_q_ref, single_k_ref, single_v_ref, bias_ref,
    earlier_ref, out_ref, score_ref,
):
    del earlier_ref
    low = low_lanes(TEXT_ROWS)
    pair_q = pair_q_ref[...].astype(F32)

    def pair_unit(head):
        return dict(
            PAIR,
            queries=jnp.where(low if head == 0 else ~low, pair_q, 0.0).astype(BF16),
            text_k=pair_k_ref[...],
            text_v=pair_v_ref[...],
            keys=lambda slot: kv_ref[slot, 2 * HD : 2 * HD + TILE, :],
            values=lambda slot: kv_ref[slot, 2 * HD + TILE :, :],
            bias=None,
        )

    single_unit = dict(
        SINGLE,
        queries=single_q_ref[...],
        text_k=single_k_ref[...],
        text_v=single_v_ref[...],
        keys=lambda slot: kv_ref[slot, :HD, :],
        values=lambda slot: kv_ref[slot, HD : 2 * HD, :],
        bias=None,
    )
    tops, totals, mixed = attend_rows([pair_unit(0), pair_unit(1), single_unit], bias_ref[...], LAYER // GROUP, score_ref)
    means = [m / t for m, t in zip(mixed, totals)]
    weighs = [top * FACTOR + jnp.log2(total) for top, total in zip(tops, totals)]
    put_text(out_ref, means, weighs)


def text_partial(kv, pair_q, pair_k, pair_v, single_q, single_k, single_v, bias, earlier):
    vmem = pl.BlockSpec(memory_space=pltpu.VMEM)
    pairs = 3 * TEXT_ROWS * (LAYER + 2) * TILE
    return pl.pallas_call(
        text_kernel,
        in_specs=[vmem] * 8 + [pl.BlockSpec(memory_space=pl.ANY)],
        out_specs=vmem,
        out_shape=jax.ShapeDtypeStruct((TEXT_KEPT, 2 * LANES), F32),
        scratch_shapes=[pltpu.VMEM((3, 2 + LAYER, TEXT_ROWS, LANES), F32)],
        compiler_params=pltpu.CompilerParams(vmem_limit_bytes=VMEM_LIMIT),
        cost_estimate=pl.CostEstimate(flops=16 * HD * pairs, bytes_accessed=4 * kv.size, transcendentals=pairs),
        name="text_partial",
    )(kv, pair_q, pair_k, pair_v, single_q, single_k, single_v, bias, earlier)


def exchange(blocks, axis):
    return lax.all_to_all(blocks, axis, split_axis=0, concat_axis=0, tiled=True)


def both_sides(layer):
    count = lax.axis_size("seq")
    up = [(i, i + 1) for i in range(count - 1)]
    down = [(i + 1, i) for i in range(count - 1)]
    return lax.ppermute(layer, "seq", up), lax.ppermute(layer, "seq", down)


def after(value, *others):
    return lax.optimization_barrier((value,) + others)[0]


def body(video_q, video_k, video_v, text_q, text_k, text_v, offsets, block_mask, text_mask):
    odd = lax.axis_index("head") % 2 == 1

    def split_text(text):
        grown = jnp.pad(text, ((0, TEXT_ROWS - TEXT), (0, 0)))
        return jnp.where(odd, grown[:, HD:], grown[:, : 2 * HD]), jnp.where(odd, grown[:, :HD], grown[:, 2 * HD :])

    (pair_tq, single_tq), (pair_tk, single_tk), (pair_tv, single_tv) = map(split_text, (text_q, text_k, text_v))
    single_tk, single_tv = single_tk.T, single_tv.T
    text_live = jnp.pad(text_mask, (0, TEXT_ROWS - TEXT)) == 1
    bias = jnp.where(text_live, 0.0, NEG_FILL).astype(F32)[None, :]
    own_bias = jnp.where(lax.axis_index("seq") == 0, bias, NEG_FILL)

    lists = neighbour_lists(offsets, block_mask)
    text = (pair_tq, pair_tk, pair_tv, single_tq, single_tk, single_tv)
    kv = exchange(pack(video_k, video_v), "head")
    kv, queries, *rest = lax.optimization_barrier((kv, pack(video_q)) + lists + text)
    lists, (pair_tq, pair_tk, pair_tv, single_tq, single_tk, single_tv) = rest[:3], rest[3:]
    queries = exchange(after(queries, kv), "head")
    single_kv = kv[:, : 2 * HD]
    single_before, single_after = both_sides(single_kv)
    token = lax.ppermute(kv[0, :16], "head", [(i, i ^ 1) for i in range(lax.axis_size("head"))])
    pair_before, pair_after = both_sides(kv[:, 2 * HD :])
    partial = text_partial(kv, pair_tq, pair_tk, pair_tv, single_tq, single_tk, single_tv, own_bias, token)
    partial = from_others(partial, 4)

    partial = merge(partial, False)
    pair_q = after(queries, partial)
    partial = from_others(partial, 1)

    pair_out = video_attention(2, lists, pair_q, HD, pair_before, kv, 2 * HD, pair_after, pair_tk, pair_tv, bias)
    pair_back = exchange(pair_out, "head")
    single_q = after(queries, pair_out)
    single_out = video_attention(
        1, lists, single_q, 0, single_before, kv, 0, single_after, single_tk, single_tv, bias
    )
    single_back = exchange(after(single_out, pair_back, *partial), "head")
    video_out = unpack(single_back, pair_back)

    pair_part, single_part = (part[:TEXT] for part in merge(partial, True))
    text_out = jnp.where(
        odd,
        jnp.concatenate([single_part, pair_part], axis=1),
        jnp.concatenate([pair_part, single_part], axis=1),
    )
    return video_out, text_out


def solution(mesh):
    return jax.shard_map(
        body,
        mesh=mesh,
        in_specs=(
            P(("seq", "head"), None),
            P(("seq", "head"), None),
            P(("seq", "head"), None),
            P(None, "head"),
            P(None, "head"),
            P(None, "head"),
            P(),
            P("seq", None),
            P(),
        ),
        out_specs=(P(("seq", "head"), None), P(None, "head")),
        check_vma=False,
    )
```
